32 devices in a mesh: grp: 4 (over z), gene: 8 (over y, x, core).
Axes of the slice: x: 2, y: 2, z: 4, core: 2. Of those that a mesh axis runs over, the one named last changes fastest.
Arguments:
- counts: int32 [1024, 7680], P('grp', 'gene'), may hold values from 0 to 12
- panels: int32 [7680], P('gene'), may hold values from 0 to 63
- membership: int32 [4, 256], P('grp'), may hold values from 0 to 3, never falling along the last dimension, each value on 1 to 128 neighbouring positions
- w_proj: bfloat16 [7680, 6400], P('gene'), may hold values from -0.03125 to 0.03125
- w_qkv_within: bfloat16 [1600, 32, 150], P(None, 'gene'), may hold values from -0.15625 to 0.15625
- w_out_within: bfloat16 [32, 50, 1600], P('gene'), may hold values from -0.4375 to 0.4375
- w_qkv_cross: bfloat16 [1600, 32, 150], P(None, 'gene'), may hold values from -0.15625 to 0.15625
- w_out_cross: bfloat16 [32, 50, 1600], P('gene'), may hold values from -0.4375 to 0.4375
- w_mean: bfloat16 [1600, 7680], P(None, 'gene'), may hold values from -0.25 to 0.25
- w_disp: bfloat16 [1600, 64], replicated, may hold values from -0.25 to 0.25
Outputs:
- cell_loss: float32 [1024], P('grp')
- grad_mean: float32 [1600, 7680], P('grp', 'gene')
- grad_disp: float32 [1600, 64], replicated
The draws below stay inside these ranges and needn't reach their ends.
Inputs may be any that keep to these rules, and one draw needn't show every extreme that they name: `membership`: group numbers never fall along a row; a group has at most 128 cells.
All inputs are finite; a program needn't handle non-finite values.
Results may differ from the reference program's by a relative error of at most 0.00055.
Values may be sent and summed in bfloat16 or wider, within the bound.
No kernel may reach another device: no remote copies, remote signals or barrier semaphores. Data moves between devices by JAX's collectives and lax.ppermute only.
A program may use at most 128 MiB of HBM per device.

```python
import math
import jax
import jax.numpy as jnp
import numpy as np
from jax import lax

D = 1600
HEADS = 32
HD = 50
MODULES = 4
PANELS = 64
CELLS_DEV = 256
GROUPS_DEV = 4
GROUP_MOST = 128
GSHARDS = 4
CELLS = 1024
GENES = 7680


def draw_counts(key, part):
    cell_key, count_key = jax.random.split(jax.random.fold_in(key, 11))
    cell_rate = jax.random.randint(cell_key, (CELLS, 1), 1, 4)
    rising = 1 + 4 * jnp.arange(GENES, dtype=jnp.int32) // GENES
    upper = 1 + cell_rate * rising[None, :]
    return jax.random.randint(count_key, (CELLS, GENES), 0, upper).astype(jnp.int32)


def decoder_draw(key, columns):
    scale = D ** (-0.5)
    values = jnp.clip(jax.random.normal(key, (D, columns), jnp.float32), -4.0, 4.0) * scale
    values = jnp.clip(values, -0.25, 0.25)
    return values.astype(jnp.bfloat16)


def draw_w_mean(key, part):
    return decoder_draw(jax.random.fold_in(key, 23), GENES)


def draw_w_disp(key, part):
    return decoder_draw(jax.random.fold_in(key, 37), PANELS)


def plant(result, stream_key, least, top_value):
    shape = result.shape
    index_at = [jax.random.randint(jax.random.fold_in(stream_key, axis), (), 0, shape[axis]) for axis in range(len(shape))]
    result = result.at[tuple(index_at)].set(least)
    longest = shape.index(max(shape))
    index_at[longest] = (index_at[longest] + 1) % shape[longest]
    return result.at[tuple(index_at)].set(top_value)


def shard_levels(stream_key, extent, pieces, least, high):
    factor_of = 1.0
    for axis_at, parts in pieces:
        steps = jax.random.uniform(jax.random.fold_in(jax.random.fold_in(stream_key, 6), axis_at), (parts,), jnp.float32, least / len(pieces), high / len(pieces))
        factor_of = factor_of * jnp.repeat(jnp.exp(steps), extent[axis_at] // parts).reshape((-1,) + (1,) * (len(extent) - 1 - axis_at))
    return factor_of


def split_up(count, total, reach, slope):
    loads = [(1 << 20) // math.isqrt(rank ** slope) + 1 for rank in range(2, count + 1)]
    rest, holding = total - reach - (count - 1), [1] * (count - 1)
    while rest > 0:
        candidates = [i for i in range(count - 1) if holding[i] < reach]
        pool, remaining = sum([loads[i] for i in candidates]), rest
        for i in candidates:
            extra = min(reach - holding[i], max(1, remaining * loads[i] // pool), rest)
            holding[i] = holding[i] + extra
            rest = rest - extra
    return np.array([reach] + holding)


def ragged(stream_key, amount, total, reach, lean):
    if amount == 2:
        one = jax.random.randint(stream_key, (), max(1, total - reach), min(reach, total - 1) + 1)
        return jnp.stack([one, total - one])
    lengths = jnp.asarray(split_up(amount, total, reach, lean), jnp.int32)
    twos = (amount - 1) // 2
    donor, sink = lengths[1:1 + 2 * twos:2], lengths[2:2 + 2 * twos:2]
    margin = jnp.minimum(donor - 1, reach - sink)
    passed = jax.random.randint(jax.random.fold_in(stream_key, 1), (twos,), 0, 1 << 20) % (margin + 1)
    lengths = lengths.at[1:1 + 2 * twos:2].set(donor - passed).at[2:2 + 2 * twos:2].set(sink + passed)
    return lengths[jax.random.permutation(jax.random.fold_in(stream_key, 2), amount)]


def noise(stream_key, shape, deviation, limit, cuts=(), kind=jnp.bfloat16):
    loudness = shard_levels(stream_key, shape, cuts, -0.22, 0.18) if cuts else 1.0
    values = jax.random.normal(stream_key, shape, jnp.float32) * deviation * loudness
    return jnp.minimum(jnp.maximum(values, -limit), limit).astype(kind)


def setup_inputs(seed: int = 0) -> dict:
    key_of = jax.random.split(jax.random.key(seed), 11)
    return {
        "counts": draw_counts(jax.random.fold_in(key_of[10], 71), 0),
        "panels": plant(jax.random.randint(key_of[1], (GENES,), 0, PANELS), jax.random.fold_in(key_of[1], 1), 0, PANELS - 1).astype(jnp.int32),
        "membership": jax.vmap(lambda own: jnp.searchsorted(jnp.cumsum(ragged(own, GROUPS_DEV, CELLS_DEV, GROUP_MOST, 0)), jnp.arange(CELLS_DEV), side="right"))(jax.random.split(key_of[2], GSHARDS)).reshape((GSHARDS, CELLS_DEV)).astype(jnp.int32),
        "w_proj": noise(key_of[3], (GENES, MODULES * D), (4 * GENES) ** -0.5, 0.03125, ((0, 8),)),
        "w_qkv_within": noise(key_of[4], (D, HEADS, 3 * HD), D ** -0.5, 0.15625, ((1, 8),)),
        "w_out_within": noise(key_of[5], (HEADS, HD, D), (4 * HD) ** -0.5, 0.4375, ((0, 8),)),
        "w_qkv_cross": noise(key_of[6], (D, HEADS, 3 * HD), D ** -0.5, 0.15625, ((1, 8),)),
        "w_out_cross": noise(key_of[7], (HEADS, HD, D), (4 * HD) ** -0.5, 0.4375, ((0, 8),)),
        "w_mean": draw_w_mean(jax.random.fold_in(key_of[10], 71), 0),
        "w_disp": draw_w_disp(jax.random.fold_in(key_of[10], 71), 0),
    }


EPS = 1e-06
FLOOR = 0.3
TARGET = 10000.0
DISP_BASE = 0.5

def rms_rows(values):
    return values * lax.rsqrt(lax.optimization_barrier(jnp.mean(values * values, axis=-1, keepdims=True)) + EPS)

def head_norm(values):
    return values * lax.rsqrt(jnp.maximum(lax.optimization_barrier(jnp.mean(values * values, axis=-1, keepdims=True)), FLOOR))

def split_heads(qkv, heads):
    qkv = qkv.reshape(qkv.shape[0], heads, 3, -1)
    query = head_norm(qkv[:, :, 0]).astype(jnp.bfloat16)
    keys = head_norm(qkv[:, :, 1]).astype(jnp.bfloat16)
    values = qkv[:, :, 2].astype(jnp.bfloat16)
    return (query, keys, values)

def within_cells(query, keys, values, modules):
    rows, heads, width = query.shape
    cells = rows // modules
    q_all = query.astype(jnp.float32).reshape(cells, modules, heads, width)
    k_all = keys.astype(jnp.float32).reshape(cells, modules, heads, width)
    v_all = values.astype(jnp.float32).reshape(cells, modules, heads, width)
    scores = jnp.einsum('cmhd,cnhd->chmn', q_all, k_all) * width ** (-0.5)
    weights = jnp.exp(scores)
    probs = (weights / lax.optimization_barrier(jnp.sum(weights, axis=-1, keepdims=True))).astype(jnp.bfloat16)
    mixed = jnp.einsum('chmn,cnhd->cmhd', probs.astype(jnp.float32), v_all)
    return mixed.astype(jnp.bfloat16).reshape(rows, heads * width)

def across_cells(query, keys, values, groups, modules):
    rows, heads, width = query.shape
    cells = rows // modules
    q_all = query.astype(jnp.float32).reshape(cells, modules, heads, width)
    k_all = keys.astype(jnp.float32).reshape(cells, modules, heads, width)
    v_all = values.astype(jnp.float32).reshape(cells, modules, heads, width)
    scores = jnp.einsum('cmhd,nmhd->mhcn', q_all, k_all) * width ** (-0.5)
    same = groups[:, None] == groups[None, :]
    weights = jnp.where(same[None, None], jnp.exp(scores), 0.0)
    probs = (weights / lax.optimization_barrier(jnp.sum(weights, axis=-1, keepdims=True))).astype(jnp.bfloat16)
    mixed = jnp.einsum('mhcn,nmhd->cmhd', probs.astype(jnp.float32), v_all)
    return mixed.astype(jnp.bfloat16).reshape(rows, heads * width)

def nb_terms(observed, rate, theta):
    total = theta + rate
    log_total = jnp.log(total)
    nll = -(lax.lgamma(observed + theta) - lax.lgamma(theta) - lax.lgamma(observed + 1.0) + theta * (jnp.log(theta) - log_total) + observed * (jnp.log(rate) - log_total))
    d_rate = (theta + observed) / total - observed / rate
    d_theta = -(lax.digamma(observed + theta) - lax.digamma(theta) + jnp.log(theta) + 1.0 - log_total - (theta + observed) / total)
    return (nll, d_rate, d_theta)

def reference(counts, panels, membership, w_proj, w_qkv_within, w_out_within, w_qkv_cross, w_out_cross, w_mean, w_disp):
    flat_within = w_qkv_within.reshape(D, -1)
    flat_cross = w_qkv_cross.reshape(D, -1)
    out_within = w_out_within.reshape(HEADS * HD, D)
    out_cross = w_out_cross.reshape(HEADS * HD, D)

    def encode(block):
        counts_block, groups = block
        observed = counts_block.astype(jnp.float32)
        library = 1.0 + lax.optimization_barrier(jnp.sum(observed, axis=1))
        scaled = jnp.log1p(observed * (TARGET / library)[:, None]).astype(jnp.bfloat16)
        tokens = jnp.dot(scaled, w_proj, preferred_element_type=jnp.float32).reshape(CELLS_DEV * MODULES, D)
        normed = rms_rows(tokens).astype(jnp.bfloat16)
        query, keys, values = split_heads(jnp.dot(normed, flat_within, preferred_element_type=jnp.float32), HEADS)
        mixed = within_cells(query, keys, values, MODULES)
        tokens = tokens + jnp.dot(mixed, out_within, preferred_element_type=jnp.float32)
        normed = rms_rows(tokens).astype(jnp.bfloat16)
        query, keys, values = split_heads(jnp.dot(normed, flat_cross, preferred_element_type=jnp.float32), HEADS)
        mixed = across_cells(query, keys, values, groups, MODULES)
        tokens = tokens + jnp.dot(mixed, out_cross, preferred_element_type=jnp.float32)
        pooled = lax.optimization_barrier(jnp.mean(tokens.reshape(CELLS_DEV, MODULES, D), axis=1))
        return (rms_rows(pooled).astype(jnp.bfloat16), library)
    hidden, library = lax.map(encode, (counts.reshape(GSHARDS, CELLS_DEV, GENES), membership))
    hidden = hidden.reshape(CELLS, D)
    library = library.reshape(CELLS)
    observed = counts.astype(jnp.float32)
    logit = jnp.dot(hidden, w_mean, preferred_element_type=jnp.float32)
    disp = jnp.dot(hidden, w_disp, preferred_element_type=jnp.float32)
    onehot = (panels[None, :] == jnp.arange(PANELS, dtype=jnp.int32)[:, None]).astype(jnp.float32)
    theta = jnp.dot(DISP_BASE + jax.nn.softplus(disp), onehot, precision=lax.Precision.HIGHEST)
    rate_scale = (library / GENES)[:, None]
    rate = rate_scale * jax.nn.softplus(logit)
    nll, d_rate, d_theta = nb_terms(observed, rate, theta)
    norm_scale = CELLS ** (-0.5)
    cell_loss = lax.optimization_barrier(jnp.sum(nll, axis=1)) / GENES
    d_logit = d_rate * rate_scale * jax.nn.sigmoid(logit) * norm_scale
    d_panel = jnp.dot(d_theta, onehot.T, precision=lax.Precision.HIGHEST)
    d_disp = d_panel * jax.nn.sigmoid(disp) * norm_scale
    hidden_f = hidden.astype(jnp.float32)
    dims = (((0,), (0,)), ((), ()))
    grad_mean = lax.dot_general(hidden_f, d_logit, dims, precision=lax.Precision.HIGHEST)
    grad_disp = lax.dot_general(hidden_f, d_disp, dims, precision=lax.Precision.HIGHEST)
    return (cell_loss, grad_mean, grad_disp)
```

```python
import functools

import jax
import jax.numpy as jnp
from jax import lax
from jax.experimental import pallas as pl
from jax.experimental.pallas import tpu as pltpu
from jax.sharding import PartitionSpec as P

EPS = 1e-06
FLOOR = 0.3
TARGET = 10000.0
DISP_BASE = 0.5
COUNT_MOST = 12
LANES = 128
EXTRA = 16
LOG2_E = 1.4426950408889634

F32 = jnp.float32
BF16 = jnp.bfloat16
NT = (((1,), (1,)), ((), ()))
PARAMS = pltpu.CompilerParams(vmem_limit_bytes=12 * 1024 * 1024)
LARGE = pltpu.CompilerParams(vmem_limit_bytes=20 * 1024 * 1024)
WHOLE = pl.BlockSpec(memory_space=pltpu.VMEM)
SCALAR = pl.BlockSpec(memory_space=pltpu.SMEM)
UNREAD = pl.BlockSpec(memory_space=pl.ANY)


def shape_of(shape, dtype):
    return jax.ShapeDtypeStruct(shape, dtype)


def launch(kernel, args, in_specs, after=(), params=PARAMS, **options):
    count = len(args)

    def body(*refs):
        kernel(*refs[:count], *refs[count + len(after) :])

    return pl.pallas_call(
        body,
        in_specs=list(in_specs) + [UNREAD] * len(after),
        compiler_params=params,
        **options,
    )(*args, *after)


def fixed(*shape):
    return pl.BlockSpec(shape, lambda i: (0,) * len(shape))


def dot_nt(left, right):
    return lax.dot_general(left, right, NT, preferred_element_type=F32)


def dot_nn(left, right):
    return jnp.dot(left, right, preferred_element_type=F32)


def split2(value):
    high = value.astype(BF16)
    return high, (value - high.astype(F32)).astype(BF16)


def split3(value):
    high = value.astype(BF16)
    rest = value - high.astype(F32)
    middle = rest.astype(BF16)
    return high, middle, (rest - middle.astype(F32)).astype(BF16)


def softplus(value):
    return jnp.maximum(value, 0.0) + jnp.log1p(jnp.exp(-jnp.abs(value)))


def softplus_pair(value):
    small = jnp.exp(-jnp.abs(value))
    soft = jnp.maximum(value, 0.0) + jnp.log1p(small)
    return soft, jnp.where(value >= 0.0, 1.0, small) / (1.0 + small)


def sigmoid(value):
    return 1.0 / (1.0 + jnp.exp(-value))


def rms_rows(values):
    return values * lax.rsqrt(jnp.mean(values * values, axis=-1, keepdims=True) + EPS)


def tile_of(extent, unit, most):
    for tile in range(min(most, extent) // unit * unit, 0, -unit):
        if extent % tile == 0:
            return tile
    return extent


def hop(value, axis, key):
    size = lax.axis_size(axis)
    return lax.ppermute(value, axis, [(i, i ^ key[i & 1]) for i in range(size)])


def straight(mask):
    return (mask, mask)


def far_keys(size):
    masks = [1 << bit for bit in range(1, size.bit_length() - 1)]
    return list(zip(masks, masks[::-1]))


def spread_keys(size):
    keys = [(0, 0)]
    for even, odd in far_keys(size):
        keys += [(e ^ even, o ^ odd) for e, o in keys]
    return keys + [(1 ^ o, 1 ^ e) for e, o in keys]


def spread(own, axis):
    size = lax.axis_size(axis)
    blocks = [own]
    for key in far_keys(size) + [straight(1)]:
        blocks += [hop(block, axis, key) for block in blocks]
    return blocks


def holder(me, key):
    even, odd = key
    return me ^ (even + (me & 1) * (odd - even))


def project_kernel(keys, me_ref, counts_ref, scale_ref, w_ref, keep_ref, send_ref, x_ref, flat_ref):
    share = x_ref.shape[0] // len(keys)
    half = keep_ref.shape[0]

    @pl.when(pl.program_id(0) == 0)
    def _():
        scaled = jnp.log1p(counts_ref[...].astype(F32) * scale_ref[...])
        flat_ref[...] = scaled.T.astype(BF16)
        for place, key in enumerate(keys):
            x_ref[place * share : (place + 1) * share, :] = flat_ref[
                pl.ds(holder(me_ref[0], key) * share, share), :
            ]

    part = dot_nn(x_ref[...], w_ref[...])
    keep_ref[...] = part[:half]
    send_ref[...] = part[half:]


def project(me, counts_t, scale, w_proj, keys, chunk, chunks, after):
    genes, cells = counts_t.shape
    columns = w_proj.shape[1] // chunks
    tile = tile_of(columns, LANES, 640)
    steps = columns // tile
    half = cells // 2
    out = shape_of((half, columns), F32)
    return launch(
        functools.partial(project_kernel, keys),
        (me, counts_t, scale, w_proj),
        [
            SCALAR,
            fixed(genes, cells),
            fixed(1, cells),
            pl.BlockSpec((genes, tile), lambda i: (0, chunk * steps + i)),
        ],
        after,
        grid=(steps,),
        out_shape=(out, out),
        out_specs=[pl.BlockSpec((half, tile), lambda i: (0, i))] * 2,
        scratch_shapes=[pltpu.VMEM((cells, genes), BF16), pltpu.VMEM((cells, genes), BF16)],
        cost_estimate=pl.CostEstimate(
            flops=2 * cells * genes * columns,
            bytes_accessed=genes * columns * 2 + cells * columns * 4,
            transcendentals=cells * genes,
        ),
    )


def halve_kernel(keep_ref, got_ref, stay_ref, go_ref):
    half = stay_ref.shape[0]
    total = keep_ref[...] + got_ref[...].astype(F32)
    stay_ref[...] = total[:half]
    go_ref[...] = total[half:].astype(BF16)


def halve(keep, got, after=()):
    rows, columns = keep.shape
    out = (rows // 2, columns)
    return launch(
        halve_kernel,
        (keep, got),
        [WHOLE] * 2,
        after,
        out_shape=(shape_of(out, F32), shape_of(out, BF16)),
        out_specs=[WHOLE] * 2,
        cost_estimate=pl.CostEstimate(
            flops=rows * columns, bytes_accessed=rows * columns * 11, transcendentals=0
        ),
    )


def rows_kernel(chunks, *refs):
    tokens_ref, normed_ref = refs[2 * chunks :]
    width = tokens_ref.shape[2]
    parts = tokens_ref.shape[0] // chunks
    for chunk in range(chunks):
        total = refs[2 * chunk][...] + refs[2 * chunk + 1][...].astype(F32)
        for at in range(parts):
            rows = total[:, at * width : (at + 1) * width]
            tokens_ref[chunk * parts + at] = rows
            normed_ref[chunk * parts + at] = rms_rows(rows).astype(BF16)


def to_rows(pairs, width, after):
    share, columns = pairs[0][0].shape
    shape = (len(pairs) * columns // width, share, width)
    return launch(
        functools.partial(rows_kernel, len(pairs)),
        [part for pair in pairs for part in pair],
        [WHOLE] * 2 * len(pairs),
        after,
        out_shape=(shape_of(shape, F32), shape_of(shape, BF16)),
        out_specs=[WHOLE] * 2,
        cost_estimate=pl.CostEstimate(
            flops=12 * share * columns, bytes_accessed=share * columns * 24, transcendentals=0
        ),
    )


def attend_kernel(pieces, heads, head_width, w_ref, row_ref, col_ref, *refs):
    blocks = refs[:-5]
    out_ref, x_ref, query_ref, keys_ref, values_ref = refs[-5:]
    modules, share, _ = blocks[0].shape
    used = heads * head_width
    lane = lax.broadcasted_iota(jnp.int32, (1, used), 1)
    picks = [(lax.rem(lane, heads) == h).astype(F32).astype(BF16) for h in range(heads)]
    down = lax.rem(lax.broadcasted_iota(jnp.int32, (used, used), 0), heads)
    over = lax.rem(lax.broadcasted_iota(jnp.int32, (used, used), 1), heads)
    same_head = (down == over).astype(F32).astype(BF16)

    def head_norm(values):
        high, low = split2(values * values)
        mean = (dot_nn(high, same_head) + dot_nn(low, same_head)) * (1.0 / head_width)
        return (values * lax.rsqrt(jnp.maximum(mean, FLOOR))).astype(BF16)

    rows = len(pieces[0]) * share
    for at, piece in enumerate(pieces):
        for place, (block, module) in enumerate(piece):
            x_ref[at * rows + place * share : at * rows + (place + 1) * share, :] = blocks[block][
                module
            ]
    every = x_ref.shape[0]
    step = min(every, 256)
    for at in range(0, every, step):
        part = slice(at, at + step)
        qkv = dot_nt(x_ref[part, :], w_ref[...])
        query_ref[part, :] = head_norm(qkv[:, :used])
        keys_ref[part, :] = head_norm(qkv[:, used : 2 * used])
        values_ref[part, :] = qkv[:, 2 * used :].astype(BF16)
    same = row_ref[...] == col_ref[...]
    scale = head_width ** (-0.5) * LOG2_E
    for at, piece in enumerate(pieces):
        part = slice(at * rows, (at + 1) * rows)
        query, keys, values = query_ref[part, :], keys_ref[part, :], values_ref[part, :]
        mixed = jnp.zeros((rows, used), F32)
        for pick in picks:
            weights = jnp.where(same, jnp.exp2(dot_nt(query * pick, keys) * scale), 0.0)
            probs = weights * (1.0 / jnp.sum(weights, axis=-1, keepdims=True))
            mixed = mixed + dot_nn(probs.astype(BF16), values * pick)
        mixed = mixed.astype(BF16)
        for place, (block, module) in enumerate(piece):
            out_ref[block, module * share : (module + 1) * share, :] = mixed[
                place * share : (place + 1) * share
            ]


def attend(blocks, w_flat, ids, pieces, heads, head_width, after):
    count = len(blocks)
    modules, share, width = blocks[0].shape
    rows = len(pieces[0]) * share
    every = len(pieces) * rows
    used = heads * head_width
    return launch(
        functools.partial(attend_kernel, pieces, heads, head_width),
        (w_flat, *ids, *blocks),
        [WHOLE] * (3 + len(blocks)),
        after,
        out_shape=shape_of((count, modules * share, used), BF16),
        out_specs=WHOLE,
        scratch_shapes=[pltpu.VMEM((every, width), BF16)] + [pltpu.VMEM((every, used), BF16)] * 3,
        cost_estimate=pl.CostEstimate(
            flops=2 * every * (width * 3 * used + 2 * heads * rows * used),
            bytes_accessed=every * width * 2 + 3 * used * width * 2 + every * used * 2,
            transcendentals=every * rows * heads,
        ),
    )


def add_mixed(places, keys, me_ref, w_ref, resid_ref, mixed_refs):
    modules, share, _ = resid_ref.shape
    total = None
    for place, key in zip(places, keys):
        mixed = mixed_refs[0][0] if place == 0 else mixed_refs[place][...]
        term = dot_nn(mixed, w_ref[holder(me_ref[0], key)])
        total = term if total is None else total + term
    return [resid_ref[m] + total[m * share : (m + 1) * share] for m in range(modules)]


def out_kernel(places, keys, me_ref, w_ref, resid_ref, *refs):
    mid_ref, normed_ref = refs[-2:]
    for m, rows in enumerate(add_mixed(places, keys, me_ref, w_ref, resid_ref, refs[:-2])):
        mid_ref[m] = rows
        normed_ref[m] = rms_rows(rows).astype(BF16)


def pool_kernel(places, keys, me_ref, w_ref, resid_ref, *refs):
    modules = add_mixed(places, keys, me_ref, w_ref, resid_ref, refs[:-1])
    pooled = functools.reduce(jnp.add, modules) * (1.0 / len(modules))
    refs[-1][...] = rms_rows(pooled).astype(BF16)


def out_call(kernel, me, keys, mixed, w_all, resid, out_shape, after=()):
    back = [(o, e) if e & 1 else (e, o) for e, o in keys]
    _, rows, inner = mixed[0].shape
    width = w_all.shape[-1]
    return launch(
        functools.partial(kernel, [back.index(key) for key in keys], keys),
        (me, w_all, resid, *mixed),
        [SCALAR, WHOLE, WHOLE, fixed(1, rows, inner)] + [WHOLE] * (len(mixed) - 1),
        after,
        grid=(1,),
        out_shape=out_shape,
        out_specs=[WHOLE] * len(out_shape),
        cost_estimate=pl.CostEstimate(
            flops=2 * rows * len(keys) * inner * width,
            bytes_accessed=len(keys) * inner * (width + rows) * 2 + rows * width * 10,
            transcendentals=0,
        ),
    )


def panel_table(w_disp_ref, hidden, with_log):
    base = DISP_BASE + softplus(dot_nt(w_disp_ref[...], hidden))
    parts = split3(base)
    if with_log:
        parts = [jnp.concatenate(pair, axis=1) for pair in zip(parts, split3(jnp.log(base)))]
    return jnp.concatenate([p.astype(F32) for p in parts], axis=0).astype(BF16)


def panel_pick(panel_ref, panel_count):
    genes = panel_ref.shape[0]
    over = lax.rem(lax.broadcasted_iota(jnp.int32, (genes, 3 * panel_count), 1), panel_count)
    return (panel_ref[...] == over).astype(F32).astype(BF16)


def place_cells(keys, me, blocks, hid_ref):
    share = blocks[0].shape[0]
    for key, block in zip(keys, blocks):
        hid_ref[pl.ds(holder(me, key) * share, share), :] = block


def rate_terms(logit, rate_scale, theta, seen, norm):
    soft, d_soft = softplus_pair(logit)
    rate = rate_scale * soft
    total = theta + rate
    d_logit = theta * (rate - seen) * norm * d_soft / (soft * total)
    return rate, total, d_logit


def decode_kernel(
    keys, norm, me_ref, counts_ref, col_ref, row_ref, scale_ref, wm_ref, wd_ref, *refs
):
    hids = refs[: len(keys)]
    high_ref, low_ref, sum_ref, hid_ref, table_ref = refs[len(keys) :]
    cells = hid_ref.shape[0]
    panel_count = wd_ref.shape[0]

    @pl.when(pl.program_id(0) == 0)
    def _():
        place_cells(keys, me_ref[0], [block[...] for block in hids], hid_ref)
        table_ref[...] = panel_table(wd_ref, hid_ref[...], True)
        sum_ref[...] = jnp.zeros_like(sum_ref)

    both = dot_nn(panel_pick(col_ref, panel_count), table_ref[...])
    theta, log_theta = both[:, :cells], both[:, cells:]
    seen = counts_ref[...].astype(F32)
    rate, total, d_logit = rate_terms(
        dot_nt(wm_ref[...], hid_ref[...]), scale_ref[...], theta, seen, norm
    )
    high_ref[...], low_ref[...] = split2(d_logit)
    log_total = jnp.log(total)
    product = jnp.ones_like(theta)
    slope = jnp.zeros_like(theta)
    for k in range(COUNT_MOST):
        inverse = 1.0 / (k + 1.0)
        factor = theta * inverse + k * inverse
        here = seen > k
        slope = jnp.where(here, slope * factor + product * inverse, slope)
        product = jnp.where(here, product * factor, product)
    nll = -(
        jnp.log(product)
        + theta * (log_theta - log_total)
        + seen * (jnp.log(rate) - log_total)
    )
    d_theta = -(slope / product + log_theta + 1.0 - log_total - (theta + seen) / total)
    down = lax.broadcasted_iota(jnp.int32, (panel_count, theta.shape[0]), 0)
    pick = (down == row_ref[0]).astype(F32).astype(BF16)
    high, middle, low = split3(d_theta)
    sum_ref[:panel_count, :] += dot_nn(pick, high) + dot_nn(pick, middle) + dot_nn(pick, low)
    sum_ref[panel_count : panel_count + 1, :] += jnp.sum(nll, axis=0, keepdims=True)


def decode(me, keys, counts_t, panel_col, panel_row, rate_scale, w_mean_t, w_disp_t, hids, norm):
    genes, cells = counts_t.shape
    width = w_mean_t.shape[1]
    panel_count = w_disp_t.shape[0]
    steps, _, tile = panel_row.shape
    wide = -(-(panel_count + 1) // 8) * 8
    by_gene = lambda columns: pl.BlockSpec((tile, columns), lambda i: (i, 0))
    return launch(
        functools.partial(decode_kernel, keys, norm),
        (
            me,
            counts_t,
            panel_col,
            panel_row,
            rate_scale,
            w_mean_t,
            w_disp_t,
            *hids,
        ),
        [
            SCALAR,
            by_gene(cells),
            by_gene(1),
            pl.BlockSpec((1, 1, tile), lambda i: (i, 0, 0)),
            fixed(1, cells),
            by_gene(width),
            fixed(panel_count, width),
        ]
        + [fixed(*hids[0].shape)] * len(hids),
        grid=(steps,),
        out_shape=(
            shape_of((genes, cells), BF16),
            shape_of((genes, cells), BF16),
            shape_of((wide, cells), F32),
            shape_of((cells, width), BF16),
        ),
        out_specs=[by_gene(cells), by_gene(cells), fixed(wide, cells), fixed(cells, width)],
        scratch_shapes=[pltpu.VMEM((3 * panel_count, 2 * cells), BF16)],
        cost_estimate=pl.CostEstimate(
            flops=2 * genes * cells * width + 150 * genes * cells,
            bytes_accessed=genes * (width * 2 + cells * 8),
            transcendentals=8 * genes * cells,
        ),
    )


def far_kernel(keys, norm, genes_all, me_ref, first_ref, last_ref, col_ref, wm_ref, wd_ref, *refs):
    hids = refs[:2]
    high_ref, low_ref, hid_ref, table_ref = refs[2:]
    tile = wm_ref.shape[0]
    first_steps = first_ref.shape[0] // tile
    step = pl.program_id(0)
    late = jnp.maximum(step - first_steps, 0)
    early = jnp.minimum(step, first_steps - 1)
    first = first_ref[pl.ds(pl.multiple_of(early * tile, 16), tile), :].astype(F32)
    last = last_ref[pl.ds(pl.multiple_of(late * tile, 16), tile), :].astype(F32)
    seen = jnp.where(step < first_steps, first, last)
    lib = last_ref[last_ref.shape[0] - EXTRA :, :].astype(F32)
    panel_count = wd_ref.shape[0]

    @pl.when(pl.program_id(0) == 0)
    def _():
        blocks = [half[at, 0] for half in hids for at in range(half.shape[0])]
        place_cells(keys, me_ref[0], blocks, hid_ref)
        table_ref[...] = panel_table(wd_ref, hid_ref[...], False)

    library = jnp.sum(lib, axis=0, keepdims=True)
    _, _, d_logit = rate_terms(
        dot_nt(wm_ref[...], hid_ref[...]),
        library / genes_all,
        dot_nn(panel_pick(col_ref, panel_count), table_ref[...]),
        seen,
        norm,
    )
    high_ref[...], low_ref[...] = split2(d_logit)


def far_call(me, keys, other, seen, panel_col, w_mean_t, w_disp_t, hids, norm, genes_all):
    genes, width = w_mean_t.shape
    cells = seen[0].shape[1]
    panel_count = w_disp_t.shape[0]
    near, _, share, _ = hids[0].shape
    tile = tile_of(genes, 16, min(256, genes // 2))
    by_gene = lambda columns: pl.BlockSpec((tile, columns), lambda i: (i, 0))
    return launch(
        functools.partial(far_kernel, keys, norm, genes_all),
        (me, *seen, panel_col, w_mean_t, w_disp_t, *hids),
        [
            SCALAR,
            WHOLE,
            WHOLE,
            by_gene(1),
            by_gene(width),
            fixed(panel_count, width),
        ]
        + [pl.BlockSpec((near, 1, share, width), lambda i: (0, other, 0, 0))] * len(hids),
        grid=(genes // tile,),
        out_shape=(
            shape_of((genes, cells), BF16),
            shape_of((genes, cells), BF16),
            shape_of((cells, width), BF16),
        ),
        out_specs=[by_gene(cells), by_gene(cells), fixed(cells, width)],
        scratch_shapes=[pltpu.VMEM((3 * panel_count, cells), BF16)],
        cost_estimate=pl.CostEstimate(
            flops=2 * genes * cells * width + 60 * genes * cells,
            bytes_accessed=genes * (width * 2 + cells * 6),
            transcendentals=4 * genes * cells,
        ),
    )


def grad_kernel(place_ref, *refs):
    out_ref = refs[-1]
    mine, width = out_ref.shape[0], refs[0].shape[1]
    down = lax.broadcasted_iota(jnp.int32, (mine, width), 0) + place_ref[1] * mine
    over = lax.broadcasted_iota(jnp.int32, (mine, width), 1)
    pick = (down == over).astype(F32).astype(BF16)
    total = None
    for at in range(0, len(refs) - 1, 3):
        hidden = dot_nt(pick, refs[at][...]).astype(BF16)
        term = dot_nt(hidden, refs[at + 1][...]) + dot_nt(hidden, refs[at + 2][...])
        total = term if total is None else total + term
    out_ref[...] = total


def grad_mean_call(place, groups):
    cells, width = groups[0][0].shape
    genes = groups[0][1].shape[0]
    mine = width // len(groups)
    return launch(
        grad_kernel,
        (place, *[array for group in groups for array in group]),
        [SCALAR] + [WHOLE] * 3 * len(groups),
        params=LARGE,
        out_shape=shape_of((mine, genes), F32),
        out_specs=WHOLE,
        cost_estimate=pl.CostEstimate(
            flops=2 * len(groups) * cells * mine * (width + 2 * genes),
            bytes_accessed=len(groups) * cells * (width + 2 * genes) * 2 + mine * genes * 4,
            transcendentals=0,
        ),
    )


def disp_kernel(norm, genes_all, place_ref, wd_ref, *refs):
    count = (len(refs) - 3) // 2
    sums, hids = refs[:count], refs[count : 2 * count]
    grad_ref, loss_ref, term_ref = refs[2 * count :]
    panel_count = wd_ref.shape[0]
    for other in range(count):
        hidden = hids[other][...]
        d_disp = sums[other][:panel_count] * sigmoid(dot_nt(wd_ref[...], hidden)) * norm
        high, middle, low = split3(d_disp)
        term_ref[place_ref[1] ^ other] = (
            dot_nn(high, hidden) + dot_nn(middle, hidden) + dot_nn(low, hidden)
        )
    total = term_ref[0]
    for block in range(1, count):
        total = total + term_ref[block]
    grad_ref[...] = total
    loss_ref[...] = sums[0][panel_count : panel_count + 1] * (1.0 / genes_all)


def disp_call(place, sums, hids, w_disp_t, norm, genes_all, after):
    panel_count, width = w_disp_t.shape
    cells = sums[0].shape[1]
    return launch(
        functools.partial(disp_kernel, norm, genes_all),
        (place, w_disp_t, *sums, *hids),
        [SCALAR] + [WHOLE] * (1 + len(sums) + len(hids)),
        after,
        out_shape=(shape_of((panel_count, width), F32), shape_of((1, cells), F32)),
        out_specs=[WHOLE] * 2,
        scratch_shapes=[pltpu.VMEM((len(sums), panel_count, width), F32)],
    )


def add_kernel(left_ref, right_ref, out_ref):
    out_ref[...] = left_ref[...] + right_ref[...]


def add(left, right, after):
    return launch(
        add_kernel,
        (left, right),
        [WHOLE] * 2,
        after,
        out_shape=shape_of(left.shape, left.dtype),
        out_specs=WHOLE,
    )


def stack_kernel(*refs):
    for at, ref in enumerate(refs[:-1]):
        refs[-1][at] = ref[...]


def stack(parts, after):
    return launch(
        stack_kernel,
        parts,
        [WHOLE] * len(parts),
        after,
        out_shape=shape_of((len(parts),) + parts[0].shape, parts[0].dtype),
        out_specs=WHOLE,
    )


def flat_qkv(weights):
    return weights.transpose(2, 1, 0).reshape(-1, weights.shape[0])


def flat_out(weights):
    return weights.transpose(1, 0, 2).reshape(-1, weights.shape[2])


def shards(
    counts,
    panels,
    membership,
    w_proj,
    w_qkv_within,
    w_out_within,
    w_qkv_cross,
    w_out_cross,
    w_mean,
    w_disp,
):
    cells, genes_here = counts.shape
    width, heads, triple = w_qkv_within.shape
    head_width = triple // 3
    modules = w_proj.shape[1] // width
    gene_count = lax.axis_size("gene")
    grp_count = lax.axis_size("grp")
    genes_all = genes_here * gene_count
    share = cells // gene_count
    panel_count = w_disp.shape[1]
    norm = float(cells * grp_count) ** (-0.5)
    gene_me = lax.axis_index("gene").astype(jnp.int32)
    grp_me = lax.axis_index("grp").astype(jnp.int32)
    me = gene_me.reshape(1)
    place = jnp.stack([gene_me, grp_me])
    keys = spread_keys(gene_count)
    far = far_keys(gene_count)

    counts_t = counts.T
    w_mean_t = w_mean.T
    w_disp_t = w_disp.T

    library = jnp.sum(counts_t.astype(F32), axis=0, keepdims=True)
    for bit in range(gene_count.bit_length() - 1):
        library = library + hop(library, "gene", straight(1 << bit))
    library = 1.0 + library
    flat_within = flat_qkv(w_qkv_within)
    flat_cross = flat_qkv(w_qkv_cross)
    out_within = lax.all_gather(flat_out(w_out_within), "gene")
    out_cross = lax.all_gather(flat_out(w_out_cross), "gene")

    cell_ids = jnp.tile(jnp.arange(share, dtype=jnp.int32), modules)
    odd = (gene_me & 1) == 1
    owners = gene_me ^ jnp.where(odd, jnp.array([o for _, o in keys]), jnp.array([e for e, _ in keys]))
    group_ids = jnp.take(membership.reshape(gene_count, share), owners, axis=0).reshape(-1)
    cell_ids = (cell_ids.reshape(-1, 1), cell_ids.reshape(1, -1))
    group_ids = (group_ids.reshape(-1, 1), group_ids.reshape(1, -1))
    tile = tile_of(genes_here, 16, min(256, genes_here // 2))
    panel_col = panels.reshape(genes_here, 1)
    panel_row = panels.reshape(genes_here // tile, 1, tile)

    halves = []
    for chunk in range(2):
        early = [flat_within, flat_cross, *cell_ids, *group_ids, panel_col, panel_row]
        keep, send = project(
            me, counts_t, TARGET / library, w_proj, keys, chunk, 2, early if chunk == 0 else []
        )
        halves.append((keep, hop(send, "gene", straight(1))))
    parts = jnp.concatenate([p.astype(F32) for p in split3(library)], axis=0)
    parts = jnp.pad(parts, ((0, EXTRA - parts.shape[0]), (0, 0)))
    middle = genes_here // tile // 2 * tile
    seen_parts = [
        counts_t[:middle].astype(BF16),
        jnp.concatenate([counts_t[middle:].astype(F32), parts], axis=0).astype(BF16),
    ]
    seen = [
        [hop(part, "grp", straight(rel)) for part in seen_parts] for rel in range(1, grp_count)
    ]
    every = [part for pair in seen[1:] for part in pair]
    waits = [every[at::4] for at in range(4)] + [seen[0]]
    for key in far[::-1]:
        nexts = []
        for chunk, (keep, got) in enumerate(halves):
            keep, send = halve(keep, got)
            nexts.append((keep, hop(send, "gene", key)))
        halves = nexts
    resid, normed = to_rows(halves, width, waits[0])

    in_cell = [[(block, m) for m in range(modules)] for block in range(gene_count)]
    across = [[(block, m) for block in range(gene_count)] for m in range(modules)]

    def send_mixed(mixed):
        return [mixed] + [hop(mixed[at], "gene", keys[at]) for at in range(1, gene_count)]

    mixed = attend(
        spread(normed, "gene"), flat_within, cell_ids, in_cell, heads, head_width, waits[1]
    )
    rows = (modules, share, width)
    mid, normed = out_call(
        out_kernel,
        me,
        keys,
        send_mixed(mixed),
        out_within,
        resid,
        [shape_of(rows, F32), shape_of(rows, BF16)],
        waits[2],
    )

    mixed = attend(
        spread(normed, "gene"),
        flat_cross,
        group_ids,
        across,
        heads,
        head_width,
        waits[3],
    )
    (hidden,) = out_call(
        pool_kernel, me, keys, send_mixed(mixed), out_cross, mid, [shape_of((share, width), BF16)], waits[4]
    )

    hids = spread(hidden, "gene")
    far_hids = [stack([hop(hidden, "grp", straight(rel)) for rel in range(1, grp_count)], hids)]
    far_hids += [hop(far_hids[0], "gene", key) for key in keys[1 : gene_count // 2]]
    high, low, sums, own_hid = decode(
        me, keys, counts_t, panel_col, panel_row, library / genes_all, w_mean_t, w_disp_t, hids, norm
    )
    groups = [(own_hid, high, low)]
    far_hids = [stack(far_hids, [high])]
    far_hids.append(hop(far_hids[0], "gene", straight(1)))
    for other in range(grp_count - 1):
        high, low, hid = far_call(
            me, keys, other, seen[other], panel_col, w_mean_t, w_disp_t, far_hids, norm, genes_all
        )
        groups.append((hid, high, low))
    bits = gene_count.bit_length() - 1
    for bit in range(bits):
        after = [groups[1][1]] if bit == bits - 1 else []
        sums = add(sums, hop(sums, "gene", straight(1 << bit)), after)
    sums = [sums] + [hop(sums, "grp", straight(rel)) for rel in range(1, grp_count)]
    grad_mean = grad_mean_call(place, groups)
    grad_disp, loss = disp_call(
        place, sums, [group[0] for group in groups], w_disp_t, norm, genes_all, [grad_mean]
    )
    return (loss.reshape(cells), grad_mean, grad_disp.T)


def solution(mesh):
    return jax.shard_map(
        shards,
        mesh=mesh,
        in_specs=(
            P("grp", "gene"),
            P("gene"),
            P("grp", None),
            P("gene", None),
            P(None, "gene", None),
            P("gene", None, None),
            P(None, "gene", None),
            P("gene", None, None),
            P(None, "gene"),
            P(),
        ),
        out_specs=(P("grp"), P("grp", "gene"), P()),
        check_vma=False,
    )
```

```python
import functools

import jax
import jax.numpy as jnp
from jax import lax
from jax.experimental import pallas as pl
from jax.experimental.pallas import tpu as pltpu
from jax.sharding import PartitionSpec as P

EPS = 1e-06
FLOOR = 0.3
TARGET = 10000.0
DISP_BASE = 0.5
COUNT_MOST = 12
LANES = 128
EXTRA = 16
LOG2_E = 1.4426950408889634

F32 = jnp.float32
BF16 = jnp.bfloat16
NT = (((1,), (1,)), ((), ()))
PARAMS = pltpu.CompilerParams(vmem_limit_bytes=12 * 1024 * 1024)
LARGE = pltpu.CompilerParams(vmem_limit_bytes=20 * 1024 * 1024)
WHOLE = pl.BlockSpec(memory_space=pltpu.VMEM)
SCALAR = pl.BlockSpec(memory_space=pltpu.SMEM)
UNREAD = pl.BlockSpec(memory_space=pl.ANY)


def shape_of(shape, dtype):
    return jax.ShapeDtypeStruct(shape, dtype)


def launch(kernel, args, in_specs, after=(), params=PARAMS, **options):
    count = len(args)

    def body(*refs):
        kernel(*refs[:count], *refs[count + len(after) :])

    return pl.pallas_call(
        body,
        in_specs=list(in_specs) + [UNREAD] * len(after),
        compiler_params=params,
        **options,
    )(*args, *after)


def fixed(*shape):
    return pl.BlockSpec(shape, lambda i: (0,) * len(shape))


def dot_nt(left, right):
    return lax.dot_general(left, right, NT, preferred_element_type=F32)


def dot_nn(left, right):
    return jnp.dot(left, right, preferred_element_type=F32)


def split2(value):
    high = value.astype(BF16)
    return high, (value - high.astype(F32)).astype(BF16)


def split3(value):
    high = value.astype(BF16)
    rest = value - high.astype(F32)
    middle = rest.astype(BF16)
    return high, middle, (rest - middle.astype(F32)).astype(BF16)


def softplus(value):
    return jnp.maximum(value, 0.0) + jnp.log1p(jnp.exp(-jnp.abs(value)))


def softplus_pair(value):
    small = jnp.exp(-jnp.abs(value))
    soft = jnp.maximum(value, 0.0) + jnp.log1p(small)
    return soft, jnp.where(value >= 0.0, 1.0, small) / (1.0 + small)


def sigmoid(value):
    return 1.0 / (1.0 + jnp.exp(-value))


def rms_rows(values):
    return values * lax.rsqrt(jnp.mean(values * values, axis=-1, keepdims=True) + EPS)


def tile_of(extent, unit, most):
    for tile in range(min(most, extent) // unit * unit, 0, -unit):
        if extent % tile == 0:
            return tile
    return extent


def hop(value, axis, key):
    size = lax.axis_size(axis)
    return lax.ppermute(value, axis, [(i, i ^ key[i & 1]) for i in range(size)])


def straight(mask):
    return (mask, mask)


def far_keys(size):
    masks = [1 << bit for bit in range(1, size.bit_length() - 1)]
    return list(zip(masks, masks[::-1]))


def spread_keys(size):
    keys = [(0, 0)]
    for even, odd in far_keys(size):
        keys += [(e ^ even, o ^ odd) for e, o in keys]
    return keys + [(1 ^ o, 1 ^ e) for e, o in keys]


def spread(own, axis):
    size = lax.axis_size(axis)
    blocks = [own]
    for key in far_keys(size) + [straight(1)]:
        blocks += [hop(block, axis, key) for block in blocks]
    return blocks


def holder(me, key):
    even, odd = key
    return me ^ (even + (me & 1) * (odd - even))


def project_kernel(keys, me_ref, counts_ref, scale_ref, w_ref, keep_ref, send_ref, x_ref, flat_ref):
    share = x_ref.shape[0] // len(keys)
    half = keep_ref.shape[0]

    @pl.when(pl.program_id(0) == 0)
    def _():
        scaled = jnp.log1p(counts_ref[...].astype(F32) * scale_ref[...])
        flat_ref[...] = scaled.T.astype(BF16)
        for place, key in enumerate(keys):
            x_ref[place * share : (place + 1) * share, :] = flat_ref[
                pl.ds(holder(me_ref[0], key) * share, share), :
            ]

    part = dot_nn(x_ref[...], w_ref[...])
    keep_ref[...] = part[:half]
    send_ref[...] = part[half:]


def project(me, counts_t, scale, w_proj, keys, chunk, chunks, after):
    genes, cells = counts_t.shape
    columns = w_proj.shape[1] // chunks
    tile = tile_of(columns, LANES, 640)
    steps = columns // tile
    half = cells // 2
    out = shape_of((half, columns), F32)
    return launch(
        functools.partial(project_kernel, keys),
        (me, counts_t, scale, w_proj),
        [
            SCALAR,
            fixed(genes, cells),
            fixed(1, cells),
            pl.BlockSpec((genes, tile), lambda i: (0, chunk * steps + i)),
        ],
        after,
        grid=(steps,),
        out_shape=(out, out),
        out_specs=[pl.BlockSpec((half, tile), lambda i: (0, i))] * 2,
        scratch_shapes=[pltpu.VMEM((cells, genes), BF16), pltpu.VMEM((cells, genes), BF16)],
        cost_estimate=pl.CostEstimate(
            flops=2 * cells * genes * columns,
            bytes_accessed=genes * columns * 2 + cells * columns * 4,
            transcendentals=cells * genes,
        ),
    )


def halve_kernel(keep_ref, got_ref, stay_ref, go_ref):
    half = stay_ref.shape[0]
    total = keep_ref[...] + got_ref[...].astype(F32)
    stay_ref[...] = total[:half]
    go_ref[...] = total[half:].astype(BF16)


def halve(keep, got, after=()):
    rows, columns = keep.shape
    out = (rows // 2, columns)
    return launch(
        halve_kernel,
        (keep, got),
        [WHOLE] * 2,
        after,
        out_shape=(shape_of(out, F32), shape_of(out, BF16)),
        out_specs=[WHOLE] * 2,
        cost_estimate=pl.CostEstimate(
            flops=rows * columns, bytes_accessed=rows * columns * 11, transcendentals=0
        ),
    )


def rows_kernel(chunks, *refs):
    tokens_ref, normed_ref = refs[2 * chunks :]
    width = tokens_ref.shape[2]
    parts = tokens_ref.shape[0] // chunks
    for chunk in range(chunks):
        total = refs[2 * chunk][...] + refs[2 * chunk + 1][...].astype(F32)
        for at in range(parts):
            rows = total[:, at * width : (at + 1) * width]
            tokens_ref[chunk * parts + at] = rows
            normed_ref[chunk * parts + at] = rms_rows(rows).astype(BF16)


def to_rows(pairs, width):
    share, columns = pairs[0][0].shape
    shape = (len(pairs) * columns // width, share, width)
    return launch(
        functools.partial(rows_kernel, len(pairs)),
        [part for pair in pairs for part in pair],
        [WHOLE] * 2 * len(pairs),
        out_shape=(shape_of(shape, F32), shape_of(shape, BF16)),
        out_specs=[WHOLE] * 2,
        cost_estimate=pl.CostEstimate(
            flops=12 * share * columns, bytes_accessed=share * columns * 24, transcendentals=0
        ),
    )


def attend_kernel(pieces, heads, head_width, w_ref, row_ref, col_ref, *refs):
    blocks = refs[:-5]
    out_ref, x_ref, query_ref, keys_ref, values_ref = refs[-5:]
    modules, share, _ = blocks[0].shape
    used = heads * head_width
    lane = lax.broadcasted_iota(jnp.int32, (1, used), 1)
    picks = [(lax.rem(lane, heads) == h).astype(F32).astype(BF16) for h in range(heads)]
    down = lax.rem(lax.broadcasted_iota(jnp.int32, (used, used), 0), heads)
    over = lax.rem(lax.broadcasted_iota(jnp.int32, (used, used), 1), heads)
    same_head = (down == over).astype(F32).astype(BF16)

    def head_norm(values):
        high, low = split2(values * values)
        mean = (dot_nn(high, same_head) + dot_nn(low, same_head)) * (1.0 / head_width)
        return (values * lax.rsqrt(jnp.maximum(mean, FLOOR))).astype(BF16)

    rows = len(pieces[0]) * share
    for at, piece in enumerate(pieces):
        for place, (block, module) in enumerate(piece):
            x_ref[at * rows + place * share : at * rows + (place + 1) * share, :] = blocks[block][
                module
            ]
    every = x_ref.shape[0]
    step = min(every, 256)
    for at in range(0, every, step):
        part = slice(at, at + step)
        qkv = dot_nt(x_ref[part, :], w_ref[...])
        query_ref[part, :] = head_norm(qkv[:, :used])
        keys_ref[part, :] = head_norm(qkv[:, used : 2 * used])
        values_ref[part, :] = qkv[:, 2 * used :].astype(BF16)
    same = row_ref[...] == col_ref[...]
    scale = head_width ** (-0.5) * LOG2_E
    for at, piece in enumerate(pieces):
        part = slice(at * rows, (at + 1) * rows)
        query, keys, values = query_ref[part, :], keys_ref[part, :], values_ref[part, :]
        mixed = jnp.zeros((rows, used), F32)
        for pick in picks:
            weights = jnp.where(same, jnp.exp2(dot_nt(query * pick, keys) * scale), 0.0)
            probs = weights * (1.0 / jnp.sum(weights, axis=-1, keepdims=True))
            mixed = mixed + dot_nn(probs.astype(BF16), values * pick)
        mixed = mixed.astype(BF16)
        for place, (block, module) in enumerate(piece):
            out_ref[block, module * share : (module + 1) * share, :] = mixed[
                place * share : (place + 1) * share
            ]


def attend(blocks, w_flat, ids, pieces, heads, head_width):
    count = len(blocks)
    modules, share, width = blocks[0].shape
    rows = len(pieces[0]) * share
    every = len(pieces) * rows
    used = heads * head_width
    return launch(
        functools.partial(attend_kernel, pieces, heads, head_width),
        (w_flat, *ids, *blocks),
        [WHOLE] * (3 + len(blocks)),
        out_shape=shape_of((count, modules * share, used), BF16),
        out_specs=WHOLE,
        scratch_shapes=[pltpu.VMEM((every, width), BF16)] + [pltpu.VMEM((every, used), BF16)] * 3,
        cost_estimate=pl.CostEstimate(
            flops=2 * every * (width * 3 * used + 2 * heads * rows * used),
            bytes_accessed=every * width * 2 + 3 * used * width * 2 + every * used * 2,
            transcendentals=every * rows * heads,
        ),
    )


def add_mixed(places, keys, me_ref, w_ref, resid_ref, mixed_refs):
    modules, share, _ = resid_ref.shape
    total = None
    for place, key in zip(places, keys):
        mixed = mixed_refs[0][0] if place == 0 else mixed_refs[place][...]
        term = dot_nn(mixed, w_ref[holder(me_ref[0], key)])
        total = term if total is None else total + term
    return [resid_ref[m] + total[m * share : (m + 1) * share] for m in range(modules)]


def out_kernel(places, keys, me_ref, w_ref, resid_ref, *refs):
    mid_ref, normed_ref = refs[-2:]
    for m, rows in enumerate(add_mixed(places, keys, me_ref, w_ref, resid_ref, refs[:-2])):
        mid_ref[m] = rows
        normed_ref[m] = rms_rows(rows).astype(BF16)


def pool_kernel(places, keys, me_ref, w_ref, resid_ref, *refs):
    modules = add_mixed(places, keys, me_ref, w_ref, resid_ref, refs[:-1])
    pooled = functools.reduce(jnp.add, modules) * (1.0 / len(modules))
    refs[-1][...] = rms_rows(pooled).astype(BF16)


def out_call(kernel, me, keys, mixed, w_all, resid, out_shape, after=()):
    back = [(o, e) if e & 1 else (e, o) for e, o in keys]
    _, rows, inner = mixed[0].shape
    width = w_all.shape[-1]
    return launch(
        functools.partial(kernel, [back.index(key) for key in keys], keys),
        (me, w_all, resid, *mixed),
        [SCALAR, WHOLE, WHOLE, fixed(1, rows, inner)] + [WHOLE] * (len(mixed) - 1),
        after,
        grid=(1,),
        out_shape=out_shape,
        out_specs=[WHOLE] * len(out_shape),
        cost_estimate=pl.CostEstimate(
            flops=2 * rows * len(keys) * inner * width,
            bytes_accessed=len(keys) * inner * (width + rows) * 2 + rows * width * 10,
            transcendentals=0,
        ),
    )


def panel_table(w_disp_ref, hidden, with_log):
    base = DISP_BASE + softplus(dot_nt(w_disp_ref[...], hidden))
    parts = split3(base)
    if with_log:
        parts = [jnp.concatenate(pair, axis=1) for pair in zip(parts, split3(jnp.log(base)))]
    return jnp.concatenate([p.astype(F32) for p in parts], axis=0).astype(BF16)


def panel_pick(panel_ref, panel_count):
    genes = panel_ref.shape[0]
    over = lax.rem(lax.broadcasted_iota(jnp.int32, (genes, 3 * panel_count), 1), panel_count)
    return (panel_ref[...] == over).astype(F32).astype(BF16)


def place_cells(keys, me, blocks, hid_ref):
    share = blocks[0].shape[0]
    for key, block in zip(keys, blocks):
        hid_ref[pl.ds(holder(me, key) * share, share), :] = block


def rate_terms(logit, rate_scale, theta, seen, norm):
    soft, d_soft = softplus_pair(logit)
    rate = rate_scale * soft
    total = theta + rate
    d_logit = theta * (rate - seen) * norm * d_soft / (soft * total)
    return rate, total, d_logit


def decode_kernel(
    keys, norm, me_ref, counts_ref, col_ref, row_ref, scale_ref, wm_ref, wd_ref, *refs
):
    hids = refs[: len(keys)]
    high_ref, low_ref, sum_ref, hid_ref, table_ref = refs[len(keys) :]
    cells = hid_ref.shape[0]
    panel_count = wd_ref.shape[0]

    @pl.when(pl.program_id(0) == 0)
    def _():
        place_cells(keys, me_ref[0], [block[...] for block in hids], hid_ref)
        table_ref[...] = panel_table(wd_ref, hid_ref[...], True)
        sum_ref[...] = jnp.zeros_like(sum_ref)

    both = dot_nn(panel_pick(col_ref, panel_count), table_ref[...])
    theta, log_theta = both[:, :cells], both[:, cells:]
    seen = counts_ref[...].astype(F32)
    rate, total, d_logit = rate_terms(
        dot_nt(wm_ref[...], hid_ref[...]), scale_ref[...], theta, seen, norm
    )
    high_ref[...], low_ref[...] = split2(d_logit)
    log_total = jnp.log(total)
    product = jnp.ones_like(theta)
    slope = jnp.zeros_like(theta)
    for k in range(COUNT_MOST):
        inverse = 1.0 / (k + 1.0)
        factor = theta * inverse + k * inverse
        here = seen > k
        slope = jnp.where(here, slope * factor + product * inverse, slope)
        product = jnp.where(here, product * factor, product)
    nll = -(
        jnp.log(product)
        + theta * (log_theta - log_total)
        + seen * (jnp.log(rate) - log_total)
    )
    d_theta = -(slope / product + log_theta + 1.0 - log_total - (theta + seen) / total)
    down = lax.broadcasted_iota(jnp.int32, (panel_count, theta.shape[0]), 0)
    pick = (down == row_ref[0]).astype(F32).astype(BF16)
    high, middle, low = split3(d_theta)
    sum_ref[:panel_count, :] += dot_nn(pick, high) + dot_nn(pick, middle) + dot_nn(pick, low)
    sum_ref[panel_count : panel_count + 1, :] += jnp.sum(nll, axis=0, keepdims=True)


def decode(me, keys, counts_t, panel_col, panel_row, rate_scale, w_mean_t, w_disp_t, hids, norm):
    genes, cells = counts_t.shape
    width = w_mean_t.shape[1]
    panel_count = w_disp_t.shape[0]
    steps, _, tile = panel_row.shape
    wide = -(-(panel_count + 1) // 8) * 8
    by_gene = lambda columns: pl.BlockSpec((tile, columns), lambda i: (i, 0))
    return launch(
        functools.partial(decode_kernel, keys, norm),
        (
            me,
            counts_t,
            panel_col,
            panel_row,
            rate_scale,
            w_mean_t,
            w_disp_t,
            *hids,
        ),
        [
            SCALAR,
            by_gene(cells),
            by_gene(1),
            pl.BlockSpec((1, 1, tile), lambda i: (i, 0, 0)),
            fixed(1, cells),
            by_gene(width),
            fixed(panel_count, width),
        ]
        + [fixed(*hids[0].shape)] * len(hids),
        grid=(steps,),
        out_shape=(
            shape_of((genes, cells), BF16),
            shape_of((genes, cells), BF16),
            shape_of((wide, cells), F32),
            shape_of((cells, width), BF16),
        ),
        out_specs=[by_gene(cells), by_gene(cells), fixed(wide, cells), fixed(cells, width)],
        scratch_shapes=[pltpu.VMEM((3 * panel_count, 2 * cells), BF16)],
        cost_estimate=pl.CostEstimate(
            flops=2 * genes * cells * width + 150 * genes * cells,
            bytes_accessed=genes * (width * 2 + cells * 8),
            transcendentals=8 * genes * cells,
        ),
    )


def far_kernel(keys, other, norm, genes_all, place_ref, seen_ref, col_ref, wm_ref, wd_ref, *refs):
    hids = refs[:2]
    high_ref, low_ref, hid_ref, table_ref = refs[2:]
    tile = wm_ref.shape[0]
    genes = seen_ref.shape[1] - EXTRA
    block = place_ref[1] ^ other
    at = pl.ds(pl.multiple_of(pl.program_id(0) * tile, 16), tile)
    seen = seen_ref[block, at, :].astype(F32)
    lib = seen_ref[block, genes:, :].astype(F32)
    panel_count = wd_ref.shape[0]

    @pl.when(pl.program_id(0) == 0)
    def _():
        blocks = [half[at, 0] for half in hids for at in range(half.shape[0])]
        place_cells(keys, place_ref[0], blocks, hid_ref)
        table_ref[...] = panel_table(wd_ref, hid_ref[...], False)

    library = jnp.sum(lib, axis=0, keepdims=True)
    _, _, d_logit = rate_terms(
        dot_nt(wm_ref[...], hid_ref[...]),
        library / genes_all,
        dot_nn(panel_pick(col_ref, panel_count), table_ref[...]),
        seen,
        norm,
    )
    high_ref[...], low_ref[...] = split2(d_logit)


def far_call(place, keys, other, seen, panel_col, w_mean_t, w_disp_t, hids, norm, genes_all):
    genes, width = w_mean_t.shape
    cells = seen.shape[2]
    panel_count = w_disp_t.shape[0]
    near, _, share, _ = hids[0].shape
    tile = tile_of(genes, 16, 256)
    by_gene = lambda columns: pl.BlockSpec((tile, columns), lambda i: (i, 0))
    return launch(
        functools.partial(far_kernel, keys, other + 1, norm, genes_all),
        (place, seen, panel_col, w_mean_t, w_disp_t, *hids),
        [
            SCALAR,
            WHOLE,
            by_gene(1),
            by_gene(width),
            fixed(panel_count, width),
        ]
        + [pl.BlockSpec((near, 1, share, width), lambda i: (0, other, 0, 0))] * len(hids),
        grid=(genes // tile,),
        out_shape=(
            shape_of((genes, cells), BF16),
            shape_of((genes, cells), BF16),
            shape_of((cells, width), BF16),
        ),
        out_specs=[by_gene(cells), by_gene(cells), fixed(cells, width)],
        scratch_shapes=[pltpu.VMEM((3 * panel_count, cells), BF16)],
        cost_estimate=pl.CostEstimate(
            flops=2 * genes * cells * width + 60 * genes * cells,
            bytes_accessed=genes * (width * 2 + cells * 6),
            transcendentals=4 * genes * cells,
        ),
    )


def grad_kernel(place_ref, *refs):
    out_ref = refs[-1]
    mine, width = out_ref.shape[0], refs[0].shape[1]
    down = lax.broadcasted_iota(jnp.int32, (mine, width), 0) + place_ref[1] * mine
    over = lax.broadcasted_iota(jnp.int32, (mine, width), 1)
    pick = (down == over).astype(F32).astype(BF16)
    total = None
    for at in range(0, len(refs) - 1, 3):
        hidden = dot_nt(pick, refs[at][...]).astype(BF16)
        term = dot_nt(hidden, refs[at + 1][...]) + dot_nt(hidden, refs[at + 2][...])
        total = term if total is None else total + term
    out_ref[...] = total


def grad_mean_call(place, groups):
    cells, width = groups[0][0].shape
    genes = groups[0][1].shape[0]
    mine = width // len(groups)
    return launch(
        grad_kernel,
        (place, *[array for group in groups for array in group]),
        [SCALAR] + [WHOLE] * 3 * len(groups),
        params=LARGE,
        out_shape=shape_of((mine, genes), F32),
        out_specs=WHOLE,
        cost_estimate=pl.CostEstimate(
            flops=2 * len(groups) * cells * mine * (width + 2 * genes),
            bytes_accessed=len(groups) * cells * (width + 2 * genes) * 2 + mine * genes * 4,
            transcendentals=0,
        ),
    )


def disp_kernel(norm, genes_all, place_ref, wd_ref, *refs):
    count = (len(refs) - 3) // 2
    sums, hids = refs[:count], refs[count : 2 * count]
    grad_ref, loss_ref, term_ref = refs[2 * count :]
    panel_count = wd_ref.shape[0]
    for other in range(count):
        hidden = hids[other][...]
        d_disp = sums[other][:panel_count] * sigmoid(dot_nt(wd_ref[...], hidden)) * norm
        high, middle, low = split3(d_disp)
        term_ref[place_ref[1] ^ other] = (
            dot_nn(high, hidden) + dot_nn(middle, hidden) + dot_nn(low, hidden)
        )
    total = term_ref[0]
    for block in range(1, count):
        total = total + term_ref[block]
    grad_ref[...] = total
    loss_ref[...] = sums[0][panel_count : panel_count + 1] * (1.0 / genes_all)


def disp_call(place, sums, hids, w_disp_t, norm, genes_all, after):
    panel_count, width = w_disp_t.shape
    cells = sums[0].shape[1]
    return launch(
        functools.partial(disp_kernel, norm, genes_all),
        (place, w_disp_t, *sums, *hids),
        [SCALAR] + [WHOLE] * (1 + len(sums) + len(hids)),
        after,
        out_shape=(shape_of((panel_count, width), F32), shape_of((1, cells), F32)),
        out_specs=[WHOLE] * 2,
        scratch_shapes=[pltpu.VMEM((len(sums), panel_count, width), F32)],
    )


def pack_kernel(counts_ref, library_ref, out_ref):
    genes, cells = counts_ref.shape
    out_ref[:genes, :] = counts_ref[...].astype(F32).astype(BF16)
    parts = [part.astype(F32) for part in split3(library_ref[...])]
    parts.append(jnp.zeros((EXTRA - len(parts), cells), F32))
    out_ref[genes:, :] = jnp.concatenate(parts, axis=0).astype(BF16)


def pack(counts_t, library, after):
    genes, cells = counts_t.shape
    return launch(
        pack_kernel,
        (counts_t, library),
        [WHOLE] * 2,
        after,
        out_shape=shape_of((genes + EXTRA, cells), BF16),
        out_specs=WHOLE,
    )


def add_kernel(left_ref, right_ref, out_ref):
    out_ref[...] = left_ref[...] + right_ref[...]


def add(left, right, after):
    return launch(
        add_kernel,
        (left, right),
        [WHOLE] * 2,
        after,
        out_shape=shape_of(left.shape, left.dtype),
        out_specs=WHOLE,
    )


def stack_kernel(*refs):
    for at, ref in enumerate(refs[:-1]):
        refs[-1][at] = ref[...]


def stack(parts, after):
    return launch(
        stack_kernel,
        parts,
        [WHOLE] * len(parts),
        after,
        out_shape=shape_of((len(parts),) + parts[0].shape, parts[0].dtype),
        out_specs=WHOLE,
    )


def flat_qkv(weights):
    return weights.transpose(2, 1, 0).reshape(-1, weights.shape[0])


def flat_out(weights):
    return weights.transpose(1, 0, 2).reshape(-1, weights.shape[2])


def shards(
    counts,
    panels,
    membership,
    w_proj,
    w_qkv_within,
    w_out_within,
    w_qkv_cross,
    w_out_cross,
    w_mean,
    w_disp,
):
    cells, genes_here = counts.shape
    width, heads, triple = w_qkv_within.shape
    head_width = triple // 3
    modules = w_proj.shape[1] // width
    gene_count = lax.axis_size("gene")
    grp_count = lax.axis_size("grp")
    genes_all = genes_here * gene_count
    share = cells // gene_count
    panel_count = w_disp.shape[1]
    norm = float(cells * grp_count) ** (-0.5)
    gene_me = lax.axis_index("gene").astype(jnp.int32)
    grp_me = lax.axis_index("grp").astype(jnp.int32)
    me = gene_me.reshape(1)
    place = jnp.stack([gene_me, grp_me])
    keys = spread_keys(gene_count)
    far = far_keys(gene_count)

    counts_t = counts.T
    w_mean_t = w_mean.T
    w_disp_t = w_disp.T

    library = jnp.sum(counts_t.astype(F32), axis=0, keepdims=True)
    for bit in range(gene_count.bit_length() - 1):
        library = library + hop(library, "gene", straight(1 << bit))
    library = 1.0 + library
    flat_within = flat_qkv(w_qkv_within)
    flat_cross = flat_qkv(w_qkv_cross)
    out_within = lax.all_gather(flat_out(w_out_within), "gene")
    cell_ids = jnp.tile(jnp.arange(share, dtype=jnp.int32), modules)
    odd = (gene_me & 1) == 1
    owners = gene_me ^ jnp.where(odd, jnp.array([o for _, o in keys]), jnp.array([e for e, _ in keys]))
    group_ids = jnp.take(membership.reshape(gene_count, share), owners, axis=0).reshape(-1)
    cell_ids = (cell_ids.reshape(-1, 1), cell_ids.reshape(1, -1))
    group_ids = (group_ids.reshape(-1, 1), group_ids.reshape(1, -1))
    tile = tile_of(genes_here, 16, 256)
    panel_col = panels.reshape(genes_here, 1)
    panel_row = panels.reshape(genes_here // tile, 1, tile)

    halves = []
    for chunk in range(2):
        early = [*cell_ids, *group_ids, panel_col, panel_row]
        keep, send = project(
            me, counts_t, TARGET / library, w_proj, keys, chunk, 2, early if chunk == 0 else []
        )
        halves.append((keep, hop(send, "gene", straight(1))))
    seen = lax.all_gather(pack(counts_t, library, [halves[0][0]]), "grp")
    laid = [flat_within, flat_cross]
    for at, key in enumerate(far[::-1]):
        nexts = []
        for chunk, (keep, got) in enumerate(halves):
            keep, send = halve(keep, got, laid[chunk : chunk + 1] if at == 1 else ())
            nexts.append((keep, hop(send, "gene", key)))
        halves = nexts
    resid, normed = to_rows(halves, width)

    in_cell = [[(block, m) for m in range(modules)] for block in range(gene_count)]
    across = [[(block, m) for block in range(gene_count)] for m in range(modules)]

    def send_mixed(mixed):
        return [mixed] + [hop(mixed[at], "gene", keys[at]) for at in range(1, gene_count)]

    blocks = spread(normed, "gene")
    mixed = attend(blocks, flat_within, cell_ids, in_cell, heads, head_width)
    out_cross = stack([flat_out(w_out_cross)], [mixed])[0]
    out_cross = lax.all_gather(out_cross, "gene")
    rows = (modules, share, width)
    mid, normed = out_call(
        out_kernel,
        me,
        keys,
        send_mixed(mixed),
        out_within,
        resid,
        [shape_of(rows, F32), shape_of(rows, BF16)],
    )

    mixed = attend(
        spread(normed, "gene"),
        flat_cross,
        group_ids,
        across,
        heads,
        head_width,
    )
    (hidden,) = out_call(
        pool_kernel, me, keys, send_mixed(mixed), out_cross, mid, [shape_of((share, width), BF16)], [seen]
    )

    hids = spread(hidden, "gene")
    far_hids = [stack([hop(hidden, "grp", straight(rel)) for rel in range(1, grp_count)], hids)]
    far_hids += [hop(far_hids[0], "gene", key) for key in keys[1 : gene_count // 2]]
    high, low, sums, own_hid = decode(
        me, keys, counts_t, panel_col, panel_row, library / genes_all, w_mean_t, w_disp_t, hids, norm
    )
    groups = [(own_hid, high, low)]
    far_hids = [stack(far_hids, [high])]
    far_hids.append(hop(far_hids[0], "gene", straight(1)))
    for other in range(grp_count - 1):
        high, low, hid = far_call(
            place, keys, other, seen, panel_col, w_mean_t, w_disp_t, far_hids, norm, genes_all
        )
        groups.append((hid, high, low))
    bits = gene_count.bit_length() - 1
    for bit in range(bits):
        after = [groups[min(bit, grp_count - 1)][1]]
        sums = add(sums, hop(sums, "gene", straight(1 << bit)), after)
    sums = [sums] + [hop(sums, "grp", straight(rel)) for rel in range(1, grp_count)]
    grad_mean = grad_mean_call(place, groups)
    grad_disp, loss = disp_call(
        place, sums, [group[0] for group in groups], w_disp_t, norm, genes_all, [grad_mean]
    )
    return (loss.reshape(cells), grad_mean, grad_disp.T)


def solution(mesh):
    return jax.shard_map(
        shards,
        mesh=mesh,
        in_specs=(
            P("grp", "gene"),
            P("gene"),
            P("grp", None),
            P("gene", None),
            P(None, "gene", None),
            P("gene", None, None),
            P(None, "gene", None),
            P("gene", None, None),
            P(None, "gene"),
            P(),
        ),
        out_specs=(P("grp"), P("grp", "gene"), P()),
        check_vma=False,
    )
```

```python
import functools

import jax
import jax.numpy as jnp
from jax import lax
from jax.experimental import pallas as pl
from jax.experimental.pallas import tpu as pltpu
from jax.sharding import PartitionSpec as P

EPS = 1e-06
FLOOR = 0.3
TARGET = 10000.0
DISP_BASE = 0.5
COUNT_MOST = 12
LANES = 128
EXTRA = 16
LOG2_E = 1.4426950408889634

F32 = jnp.float32
BF16 = jnp.bfloat16
NT = (((1,), (1,)), ((), ()))
PARAMS = pltpu.CompilerParams(vmem_limit_bytes=12 * 1024 * 1024)
LARGE = pltpu.CompilerParams(vmem_limit_bytes=20 * 1024 * 1024)
WHOLE = pl.BlockSpec(memory_space=pltpu.VMEM)
SCALAR = pl.BlockSpec(memory_space=pltpu.SMEM)
ANYWHERE = pl.BlockSpec(memory_space=pl.ANY)


def in_hbm(array):
    return pltpu.with_memory_space_constraint(array, pltpu.HBM)


def shape_of(shape, dtype):
    return jax.ShapeDtypeStruct(shape, dtype)


def launch(kernel, args, in_specs, after=(), params=PARAMS, **options):
    count = len(args)

    def body(*refs):
        kernel(*refs[:count], *refs[count + len(after) :])

    return pl.pallas_call(
        body,
        in_specs=list(in_specs) + [ANYWHERE] * len(after),
        compiler_params=params,
        **options,
    )(*args, *after)


def fixed(*shape):
    return pl.BlockSpec(shape, lambda i: (0,) * len(shape))


def dot_nt(left, right):
    return lax.dot_general(left, right, NT, preferred_element_type=F32)


def dot_nn(left, right):
    return jnp.dot(left, right, preferred_element_type=F32)


def split2(value):
    high = value.astype(BF16)
    return high, (value - high.astype(F32)).astype(BF16)


def split3(value):
    high = value.astype(BF16)
    rest = value - high.astype(F32)
    middle = rest.astype(BF16)
    return high, middle, (rest - middle.astype(F32)).astype(BF16)


def softplus(value):
    return jnp.maximum(value, 0.0) + jnp.log1p(jnp.exp(-jnp.abs(value)))


def sigmoid(value):
    return 1.0 / (1.0 + jnp.exp(-value))


def rms_rows(values):
    return values * lax.rsqrt(jnp.mean(values * values, axis=-1, keepdims=True) + EPS)


def tile_of(extent, unit, most):
    for tile in range(min(most, extent) // unit * unit, 0, -unit):
        if extent % tile == 0:
            return tile
    return extent


def hop(value, axis, key):
    size = lax.axis_size(axis)
    return lax.ppermute(value, axis, [(i, i ^ key[i & 1]) for i in range(size)])


def straight(mask):
    return (mask, mask)


def far_keys(size):
    masks = [1 << bit for bit in range(1, size.bit_length() - 1)]
    return list(zip(masks, masks[::-1]))


def spread_keys(size):
    keys = [(0, 0)]
    for even, odd in far_keys(size):
        keys += [(e ^ even, o ^ odd) for e, o in keys]
    return keys + [(1 ^ o, 1 ^ e) for e, o in keys]


def spread(own, axis):
    size = lax.axis_size(axis)
    blocks = [own]
    for key in far_keys(size) + [straight(1)]:
        blocks += [hop(block, axis, key) for block in blocks]
    return blocks


def holder(me, key):
    even, odd = key
    return me ^ (even + (me & 1) * (odd - even))


def project_kernel(keys, me_ref, counts_ref, scale_ref, w_ref, keep_ref, send_ref, x_ref, flat_ref):
    share = x_ref.shape[0] // len(keys)
    half = keep_ref.shape[0]

    @pl.when(pl.program_id(0) == 0)
    def _():
        scaled = jnp.log1p(counts_ref[...].astype(F32) * scale_ref[...])
        flat_ref[...] = scaled.T.astype(BF16)
        for place, key in enumerate(keys):
            x_ref[place * share : (place + 1) * share, :] = flat_ref[
                pl.ds(holder(me_ref[0], key) * share, share), :
            ]

    part = dot_nn(x_ref[...], w_ref[...])
    keep_ref[...] = part[:half]
    send_ref[...] = part[half:]


def project(me, counts_t, scale, w_proj, keys, chunk, chunks, after):
    genes, cells = counts_t.shape
    columns = w_proj.shape[1] // chunks
    tile = tile_of(columns, LANES, 640)
    steps = columns // tile
    half = cells // 2
    out = shape_of((half, columns), F32)
    return launch(
        functools.partial(project_kernel, keys),
        (me, counts_t, scale, in_hbm(w_proj)),
        [
            SCALAR,
            fixed(genes, cells),
            fixed(1, cells),
            pl.BlockSpec((genes, tile), lambda i: (0, chunk * steps + i)),
        ],
        after,
        grid=(steps,),
        out_shape=(out, out),
        out_specs=[pl.BlockSpec((half, tile), lambda i: (0, i))] * 2,
        scratch_shapes=[pltpu.VMEM((cells, genes), BF16), pltpu.VMEM((cells, genes), BF16)],
        cost_estimate=pl.CostEstimate(
            flops=2 * cells * genes * columns,
            bytes_accessed=genes * columns * 2 + cells * columns * 4,
            transcendentals=cells * genes,
        ),
    )


def halve_kernel(keep_ref, got_ref, stay_ref, go_ref):
    half = stay_ref.shape[0]
    total = keep_ref[...] + got_ref[...].astype(F32)
    stay_ref[...] = total[:half]
    go_ref[...] = total[half:].astype(go_ref.dtype)


def halve(keep, got, after=(), dtype=BF16):
    rows, *columns = keep.shape
    out = (rows // 2, *columns)
    size = keep.size
    return launch(
        halve_kernel,
        (keep, got),
        [WHOLE] * 2,
        after,
        out_shape=(shape_of(out, F32), shape_of(out, dtype)),
        out_specs=[WHOLE] * 2,
        cost_estimate=pl.CostEstimate(
            flops=size, bytes_accessed=size * 11, transcendentals=0
        ),
    )


def rows_kernel(chunks, *refs):
    tokens_ref, normed_ref = refs[2 * chunks :]
    width = tokens_ref.shape[2]
    parts = tokens_ref.shape[0] // chunks
    for chunk in range(chunks):
        total = refs[2 * chunk][...] + refs[2 * chunk + 1][...].astype(F32)
        for at in range(parts):
            rows = total[:, at * width : (at + 1) * width]
            tokens_ref[chunk * parts + at] = rows
            normed_ref[chunk * parts + at] = rms_rows(rows).astype(BF16)


def to_rows(pairs, width):
    share, columns = pairs[0][0].shape
    shape = (len(pairs) * columns // width, share, width)
    return launch(
        functools.partial(rows_kernel, len(pairs)),
        [part for pair in pairs for part in pair],
        [WHOLE] * 2 * len(pairs),
        out_shape=(shape_of(shape, F32), shape_of(shape, BF16)),
        out_specs=[WHOLE] * 2,
        cost_estimate=pl.CostEstimate(
            flops=12 * share * columns, bytes_accessed=share * columns * 24, transcendentals=0
        ),
    )


def attend_kernel(pieces, heads, head_width, outs, w_ref, row_ref, col_ref, *refs):
    blocks = refs[: -4 - outs]
    out_refs, refs = refs[-4 - outs : -4], refs[-4:]
    x_ref, query_ref, keys_ref, values_ref = refs
    if outs == 2:
        blocks, blocks_out = blocks[:-1], blocks[-1]
    used = heads * head_width
    _, share, _ = blocks[0].shape
    rows = len(pieces[0]) * share
    places = [spot for piece in pieces for spot in piece]
    for at, (block, module) in enumerate(places):
        x_ref[at * share : (at + 1) * share, :] = blocks[block][module]
    lane = lax.broadcasted_iota(jnp.int32, (1, used), 1)
    picks = [(lax.rem(lane, heads) == h).astype(F32).astype(BF16) for h in range(heads)]
    down = lax.rem(lax.broadcasted_iota(jnp.int32, (used, used), 0), heads)
    over = lax.rem(lax.broadcasted_iota(jnp.int32, (used, used), 1), heads)
    same_head = (down == over).astype(F32).astype(BF16)

    def head_norm(values):
        high, low = split2(values * values)
        mean = (dot_nn(high, same_head) + dot_nn(low, same_head)) * (1.0 / head_width)
        return (values * lax.rsqrt(jnp.maximum(mean, FLOOR))).astype(BF16)

    every = x_ref.shape[0]
    step = min(every, 256)
    for at in range(0, every, step):
        part = slice(at, at + step)
        qkv = dot_nt(x_ref[part, :], w_ref[...])
        query_ref[part, :] = head_norm(qkv[:, :used])
        keys_ref[part, :] = head_norm(qkv[:, used : 2 * used])
        values_ref[part, :] = qkv[:, 2 * used :].astype(BF16)
    same = row_ref[...] == col_ref[...]
    scale = head_width ** (-0.5) * LOG2_E
    summed = None
    for at, piece in enumerate(pieces):
        part = slice(at * rows, (at + 1) * rows)
        query, keys, values = query_ref[part, :], keys_ref[part, :], values_ref[part, :]
        mixed = jnp.zeros((rows, used), F32)
        for pick in picks:
            weights = jnp.where(same, jnp.exp2(dot_nt(query * pick, keys) * scale), 0.0)
            probs = weights * (1.0 / jnp.sum(weights, axis=-1, keepdims=True))
            mixed = mixed + dot_nn(probs.astype(BF16), values * pick)
        mixed = mixed.astype(BF16)
        if outs == 1:
            for place, (block, module) in enumerate(piece):
                out_refs[0][block, module * share : (module + 1) * share, :] = mixed[
                    place * share : (place + 1) * share
                ]
        else:
            mixed = mixed.astype(F32)
            summed = mixed if summed is None else summed + mixed
    if outs == 2:
        w_out = blocks_out[...]
        high, middle, low = split3(summed * (1.0 / len(pieces)))
        total = dot_nn(high, w_out) + dot_nn(middle, w_out) + dot_nn(low, w_out)
        for at in range(rows // share):
            half = rows // share // 2
            out_refs[at // half][at % half] = total[at * share : (at + 1) * share]


def attend(blocks, w_flat, ids, pieces, heads, head_width, w_out=None, after=()):
    count = len(blocks)
    modules, share, width = blocks[0].shape
    rows = len(pieces[0]) * share
    every = len(pieces) * rows
    used = heads * head_width
    if w_out is None:
        last, out_shape = [], [shape_of((count, modules * share, used), BF16)]
    else:
        last, out_shape = [w_out], [shape_of((count // 2, share, width), F32)] * 2
    return launch(
        functools.partial(attend_kernel, pieces, heads, head_width, len(out_shape)),
        (w_flat, *ids, *blocks, *last),
        [WHOLE] * (3 + len(blocks) + len(last)),
        after,
        out_shape=out_shape,
        out_specs=[WHOLE] * len(out_shape),
        scratch_shapes=[pltpu.VMEM((every, width), BF16)] + [pltpu.VMEM((every, used), BF16)] * 3,
        cost_estimate=pl.CostEstimate(
            flops=2 * every * (width * 3 * used + 2 * heads * rows * used),
            bytes_accessed=every * width * 2 + 3 * used * width * 2 + every * used * 2,
            transcendentals=every * rows * heads,
        ),
    )


def add_mixed(places, keys, me_ref, w_hbm, resid_hbm, mixed_hbm, scratch):
    mixed_ref, w_ref, resid_ref, sems = scratch
    modules, share, _ = resid_ref.shape
    count = len(keys)
    copies = []
    for at, (place, key) in enumerate(zip(places, keys)):
        source = mixed_hbm[0].at[0] if place == 0 else mixed_hbm[place]
        pair = [
            pltpu.make_async_copy(source, mixed_ref.at[at], sems.at[2 * at]),
            pltpu.make_async_copy(
                w_hbm.at[holder(me_ref[0], key)], w_ref.at[at], sems.at[2 * at + 1]
            ),
        ]
        for copy in pair:
            copy.start()
        copies.append(pair)
    resid_copy = pltpu.make_async_copy(resid_hbm, resid_ref, sems.at[2 * count])
    resid_copy.start()
    total = None
    for at, pair in enumerate(copies):
        for copy in pair:
            copy.wait()
        term = dot_nn(mixed_ref[at], w_ref[at])
        total = term if total is None else total + term
    resid_copy.wait()
    return [resid_ref[m] + total[m * share : (m + 1) * share] for m in range(modules)]


def out_kernel(places, keys, me_ref, w_hbm, resid_hbm, *refs):
    mixed, (mid_ref, normed_ref), scratch = refs[:-6], refs[-6:-4], refs[-4:]
    modules = add_mixed(places, keys, me_ref, w_hbm, resid_hbm, mixed, scratch)
    for m, rows in enumerate(modules):
        mid_ref[m] = rows
        normed_ref[m] = rms_rows(rows).astype(BF16)


def pool_kernel(resid_ref, keep_ref, got_ref, hidden_ref):
    modules = resid_ref.shape[0]
    total = functools.reduce(jnp.add, [resid_ref[m] for m in range(modules)])
    pooled = total * (1.0 / modules) + (keep_ref[0] + got_ref[0])
    hidden_ref[...] = rms_rows(pooled).astype(BF16)


def pool(resid, keep, got):
    return launch(
        pool_kernel,
        (resid, keep, got),
        [WHOLE] * 3,
        out_shape=shape_of(keep.shape[1:], BF16),
        out_specs=WHOLE,
    )


def out_call(kernel, me, keys, mixed, w_all, resid, out_shape, after=()):
    back = [(o, e) if e & 1 else (e, o) for e, o in keys]
    _, rows, inner = mixed[0].shape
    width = w_all.shape[-1]
    count = len(keys)
    return launch(
        functools.partial(kernel, [back.index(key) for key in keys], keys),
        (me, in_hbm(w_all), resid, *mixed),
        [SCALAR, ANYWHERE, ANYWHERE] + [ANYWHERE] * len(mixed),
        after,
        out_shape=out_shape,
        out_specs=[WHOLE] * len(out_shape),
        scratch_shapes=[
            pltpu.VMEM((count, rows, inner), BF16),
            pltpu.VMEM(w_all.shape, BF16),
            pltpu.VMEM(resid.shape, F32),
            pltpu.SemaphoreType.DMA((2 * count + 1,)),
        ],
        cost_estimate=pl.CostEstimate(
            flops=2 * rows * count * inner * width,
            bytes_accessed=count * inner * (width + rows) * 2 + rows * width * 10,
            transcendentals=0,
        ),
    )


def panel_table(w_disp_ref, hidden, with_log):
    base = DISP_BASE + softplus(dot_nt(w_disp_ref[...], hidden))
    parts = split3(base)
    if with_log:
        parts = [jnp.concatenate(pair, axis=1) for pair in zip(parts, split3(jnp.log(base)))]
    return jnp.concatenate([p.astype(F32) for p in parts], axis=0).astype(BF16)


def panel_pick(panel_ref, panel_count):
    genes = panel_ref.shape[0]
    over = lax.rem(lax.broadcasted_iota(jnp.int32, (genes, 3 * panel_count), 1), panel_count)
    return (panel_ref[...] == over).astype(F32).astype(BF16)


def place_cells(keys, me, blocks, hid_ref):
    share = blocks[0].shape[0]
    for key, block in zip(keys, blocks):
        hid_ref[pl.ds(holder(me, key) * share, share), :] = block


def rate_terms(logit, rate_scale, theta, seen, norm):
    small = jnp.exp(-jnp.abs(logit))
    soft = jnp.maximum(logit, 0.0) + jnp.log1p(small)
    rate = rate_scale * soft
    total = theta + rate
    above = theta * (rate - seen) * jnp.where(logit >= 0.0, norm, norm * small)
    d_logit = above / (soft * total * (1.0 + small))
    return rate, total, d_logit


def decode_kernel(
    keys, norm, me_ref, counts_ref, col_ref, row_ref, scale_ref, wm_ref, wd_ref, *refs
):
    hids = refs[: len(keys)]
    high_ref, low_ref, sum_ref, hid_ref, table_ref = refs[len(keys) :]
    cells = hid_ref.shape[0]
    panel_count = wd_ref.shape[0]

    @pl.when(pl.program_id(0) == 0)
    def _():
        place_cells(keys, me_ref[0], [block[...] for block in hids], hid_ref)
        table_ref[...] = panel_table(wd_ref, hid_ref[...], True)
        sum_ref[...] = jnp.zeros_like(sum_ref)

    both = dot_nn(panel_pick(col_ref, panel_count), table_ref[...])
    theta, log_theta = both[:, :cells], both[:, cells:]
    seen = counts_ref[...].astype(F32)
    rate, total, d_logit = rate_terms(
        dot_nt(wm_ref[...], hid_ref[...]), scale_ref[...], theta, seen, norm
    )
    high_ref[...], low_ref[...] = split2(d_logit)
    log_total = jnp.log(total)
    product = jnp.ones_like(theta)
    slope = jnp.zeros_like(theta)
    for k in range(COUNT_MOST):
        inverse = 1.0 / (k + 1.0)
        factor = theta * inverse + k * inverse
        here = seen > k
        slope = jnp.where(here, slope * factor + product * inverse, slope)
        product = jnp.where(here, product * factor, product)
    nll = -(
        jnp.log(product)
        + theta * (log_theta - log_total)
        + seen * (jnp.log(rate) - log_total)
    )
    d_theta = -(slope / product + log_theta + 1.0 - log_total - (theta + seen) / total)
    down = lax.broadcasted_iota(jnp.int32, (panel_count, theta.shape[0]), 0)
    pick = (down == row_ref[0]).astype(F32).astype(BF16)
    high, middle, low = split3(d_theta)
    sum_ref[:panel_count, :] += dot_nn(pick, high) + dot_nn(pick, middle) + dot_nn(pick, low)
    sum_ref[panel_count : panel_count + 1, :] += jnp.sum(nll, axis=0, keepdims=True)


def decode(me, keys, counts_t, panel_col, panel_row, rate_scale, w_mean_t, w_disp_t, hids, norm):
    genes, cells = counts_t.shape
    width = w_mean_t.shape[1]
    panel_count = w_disp_t.shape[0]
    steps, _, tile = panel_row.shape
    wide = -(-(panel_count + 1) // 8) * 8
    by_gene = lambda columns: pl.BlockSpec((tile, columns), lambda i: (i, 0))
    return launch(
        functools.partial(decode_kernel, keys, norm),
        (
            me,
            counts_t,
            panel_col,
            panel_row,
            rate_scale,
            in_hbm(w_mean_t),
            w_disp_t,
            *hids,
        ),
        [
            SCALAR,
            by_gene(cells),
            by_gene(1),
            pl.BlockSpec((1, 1, tile), lambda i: (i, 0, 0)),
            fixed(1, cells),
            by_gene(width),
            fixed(panel_count, width),
        ]
        + [fixed(*hids[0].shape)] * len(hids),
        grid=(steps,),
        out_shape=(
            shape_of((genes, cells), BF16),
            shape_of((genes, cells), BF16),
            shape_of((wide, cells), F32),
            shape_of((cells, width), BF16),
        ),
        out_specs=[by_gene(cells), by_gene(cells), fixed(wide, cells), fixed(cells, width)],
        scratch_shapes=[pltpu.VMEM((3 * panel_count, 2 * cells), BF16)],
        cost_estimate=pl.CostEstimate(
            flops=2 * genes * cells * width + 150 * genes * cells,
            bytes_accessed=genes * (width * 2 + cells * 8),
            transcendentals=8 * genes * cells,
        ),
    )


def far_kernel(keys, other, norm, genes_all, place_ref, seen_ref, col_ref, wm_ref, wd_ref, *refs):
    hids = refs[:2]
    high_ref, low_ref, hid_ref, table_ref = refs[2:]
    tile = wm_ref.shape[0]
    genes = seen_ref.shape[1] - EXTRA
    block = place_ref[1] ^ other
    at = pl.ds(pl.multiple_of(pl.program_id(0) * tile, 16), tile)
    seen = seen_ref[block, at, :].astype(F32)
    lib = seen_ref[block, genes:, :].astype(F32)
    panel_count = wd_ref.shape[0]

    @pl.when(pl.program_id(0) == 0)
    def _():
        blocks = [half[at, 0] for half in hids for at in range(half.shape[0])]
        place_cells(keys, place_ref[0], blocks, hid_ref)
        table_ref[...] = panel_table(wd_ref, hid_ref[...], False)

    library = jnp.sum(lib, axis=0, keepdims=True)
    _, _, d_logit = rate_terms(
        dot_nt(wm_ref[...], hid_ref[...]),
        library / genes_all,
        dot_nn(panel_pick(col_ref, panel_count), table_ref[...]),
        seen,
        norm,
    )
    high_ref[...], low_ref[...] = split2(d_logit)


def far_call(place, keys, other, seen, panel_col, w_mean_t, w_disp_t, hids, norm, genes_all):
    genes, width = w_mean_t.shape
    cells = seen.shape[2]
    panel_count = w_disp_t.shape[0]
    near, _, share, _ = hids[0].shape
    tile = tile_of(genes, 16, 256)
    by_gene = lambda columns: pl.BlockSpec((tile, columns), lambda i: (i, 0))
    return launch(
        functools.partial(far_kernel, keys, other + 1, norm, genes_all),
        (place, seen, panel_col, in_hbm(w_mean_t), w_disp_t, *hids),
        [
            SCALAR,
            WHOLE,
            by_gene(1),
            by_gene(width),
            fixed(panel_count, width),
        ]
        + [pl.BlockSpec((near, 1, share, width), lambda i: (0, other, 0, 0))] * len(hids),
        grid=(genes // tile,),
        out_shape=(
            shape_of((genes, cells), BF16),
            shape_of((genes, cells), BF16),
            shape_of((cells, width), BF16),
        ),
        out_specs=[by_gene(cells), by_gene(cells), fixed(cells, width)],
        scratch_shapes=[pltpu.VMEM((3 * panel_count, cells), BF16)],
        cost_estimate=pl.CostEstimate(
            flops=2 * genes * cells * width + 60 * genes * cells,
            bytes_accessed=genes * (width * 2 + cells * 6),
            transcendentals=4 * genes * cells,
        ),
    )


def grad_kernel(place_ref, *refs):
    out_ref = refs[-1]
    mine, width = out_ref.shape[0], refs[0].shape[1]
    down = lax.broadcasted_iota(jnp.int32, (mine, width), 0) + place_ref[1] * mine
    over = lax.broadcasted_iota(jnp.int32, (mine, width), 1)
    pick = (down == over).astype(F32).astype(BF16)
    total = None
    for at in range(0, len(refs) - 1, 3):
        hidden = dot_nt(pick, refs[at][...]).astype(BF16)
        term = dot_nt(hidden, refs[at + 1][...]) + dot_nt(hidden, refs[at + 2][...])
        total = term if total is None else total + term
    out_ref[...] = total


def grad_mean_call(place, groups):
    cells, width = groups[0][0].shape
    genes = groups[0][1].shape[0]
    mine = width // len(groups)
    return launch(
        grad_kernel,
        (place, *[array for group in groups for array in group]),
        [SCALAR] + [WHOLE] * 3 * len(groups),
        params=LARGE,
        out_shape=shape_of((mine, genes), F32),
        out_specs=WHOLE,
        cost_estimate=pl.CostEstimate(
            flops=2 * len(groups) * cells * mine * (width + 2 * genes),
            bytes_accessed=len(groups) * cells * (width + 2 * genes) * 2 + mine * genes * 4,
            transcendentals=0,
        ),
    )


def disp_kernel(norm, genes_all, place_ref, wd_ref, *refs):
    count = (len(refs) - 3) // 2
    sums, hids = refs[:count], refs[count : 2 * count]
    grad_ref, loss_ref, term_ref = refs[2 * count :]
    panel_count = wd_ref.shape[0]
    for other in range(count):
        hidden = hids[other][...]
        d_disp = sums[other][:panel_count] * sigmoid(dot_nt(wd_ref[...], hidden)) * norm
        parts = jnp.concatenate([part.astype(F32) for part in split3(d_disp)], axis=0)
        three = dot_nn(parts.astype(BF16), hidden)
        term_ref[place_ref[1] ^ other] = (
            three[:panel_count]
            + three[panel_count : 2 * panel_count]
            + three[2 * panel_count :]
        )
    total = term_ref[0]
    for block in range(1, count):
        total = total + term_ref[block]
    grad_ref[...] = total
    loss_ref[...] = sums[0][panel_count : panel_count + 1] * (1.0 / genes_all)


def disp_call(place, sums, hids, w_disp_t, norm, genes_all, after):
    panel_count, width = w_disp_t.shape
    cells = sums[0].shape[1]
    return launch(
        functools.partial(disp_kernel, norm, genes_all),
        (place, w_disp_t, *sums, *hids),
        [SCALAR] + [WHOLE] * (1 + len(sums) + len(hids)),
        after,
        out_shape=(shape_of((panel_count, width), F32), shape_of((1, cells), F32)),
        out_specs=[WHOLE] * 2,
        scratch_shapes=[pltpu.VMEM((len(sums), panel_count, width), F32)],
    )


def pack_kernel(counts_ref, library_ref, out_ref):
    genes, cells = counts_ref.shape
    out_ref[:genes, :] = counts_ref[...].astype(F32).astype(BF16)
    parts = [part.astype(F32) for part in split3(library_ref[...])]
    parts.append(jnp.zeros((EXTRA - len(parts), cells), F32))
    out_ref[genes:, :] = jnp.concatenate(parts, axis=0).astype(BF16)


def pack(counts_t, library, after):
    genes, cells = counts_t.shape
    return launch(
        pack_kernel,
        (counts_t, library),
        [WHOLE] * 2,
        after,
        out_shape=shape_of((genes + EXTRA, cells), BF16),
        out_specs=WHOLE,
    )


def add_kernel(left_ref, right_ref, out_ref):
    out_ref[...] = left_ref[...] + right_ref[...]


def add(left, right, after):
    return launch(
        add_kernel,
        (left, right),
        [WHOLE] * 2,
        after,
        out_shape=shape_of(left.shape, left.dtype),
        out_specs=WHOLE,
    )


def stack_kernel(*refs):
    for at, ref in enumerate(refs[:-1]):
        refs[-1][at] = ref[...]


def stack(parts, after):
    return launch(
        stack_kernel,
        parts,
        [WHOLE] * len(parts),
        after,
        out_shape=shape_of((len(parts),) + parts[0].shape, parts[0].dtype),
        out_specs=WHOLE,
    )


def flat_qkv(weights):
    return weights.transpose(2, 1, 0).reshape(-1, weights.shape[0])


def flat_out(weights):
    return weights.transpose(1, 0, 2).reshape(-1, weights.shape[2])


def shards(
    counts,
    panels,
    membership,
    w_proj,
    w_qkv_within,
    w_out_within,
    w_qkv_cross,
    w_out_cross,
    w_mean,
    w_disp,
):
    cells, genes_here = counts.shape
    width, heads, triple = w_qkv_within.shape
    head_width = triple // 3
    modules = w_proj.shape[1] // width
    gene_count = lax.axis_size("gene")
    grp_count = lax.axis_size("grp")
    genes_all = genes_here * gene_count
    share = cells // gene_count
    panel_count = w_disp.shape[1]
    norm = float(cells * grp_count) ** (-0.5)
    gene_me = lax.axis_index("gene").astype(jnp.int32)
    grp_me = lax.axis_index("grp").astype(jnp.int32)
    me = gene_me.reshape(1)
    place = jnp.stack([gene_me, grp_me])
    keys = spread_keys(gene_count)
    far = far_keys(gene_count)

    counts_t = counts.T
    w_mean_t = w_mean.T
    w_disp_t = w_disp.T

    library = jnp.sum(counts_t.astype(F32), axis=0, keepdims=True)
    for bit in range(gene_count.bit_length() - 1):
        library = library + hop(library, "gene", straight(1 << bit))
    library = 1.0 + library
    flat_within = flat_qkv(w_qkv_within)
    flat_cross = flat_qkv(w_qkv_cross)
    out_within = in_hbm(lax.all_gather(flat_out(w_out_within), "gene"))
    out_cross = flat_out(w_out_cross)
    cell_ids = jnp.tile(jnp.arange(share, dtype=jnp.int32), modules)
    odd = (gene_me & 1) == 1
    owners = gene_me ^ jnp.where(odd, jnp.array([o for _, o in keys]), jnp.array([e for e, _ in keys]))
    group_ids = jnp.take(membership.reshape(gene_count, share), owners, axis=0).reshape(-1)
    cell_ids = (cell_ids.reshape(-1, 1), cell_ids.reshape(1, -1))
    group_ids = (group_ids.reshape(-1, 1), group_ids.reshape(1, -1))
    tile = tile_of(genes_here, 16, 256)
    panel_col = panels.reshape(genes_here, 1)
    panel_row = panels.reshape(genes_here // tile, 1, tile)

    halves = []
    early = [*cell_ids, *group_ids, panel_col, panel_row]
    for chunk in range(2):
        keep, send = project(me, counts_t, TARGET / library, w_proj, keys, chunk, 2, early)
        early = []
        halves.append((keep, hop(send, "gene", straight(1))))
    laid = [[flat_within], [flat_cross, out_cross]]
    for at, key in enumerate(far[::-1]):
        nexts = []
        for chunk, (keep, got) in enumerate(halves):
            keep, send = halve(keep, got, laid[chunk] if at == 1 else ())
            nexts.append((keep, hop(send, "gene", key)))
        halves = nexts
    resid, normed = to_rows(halves, width)

    packed = pack(counts_t, library, [resid])
    seen = in_hbm(lax.all_gather(packed, "grp"))
    normed = stack([normed], [out_within, packed])[0]

    in_cell = [[(block, m) for m in range(modules)] for block in range(gene_count)]
    across = [[(block, m) for block in range(gene_count)] for m in range(modules)]

    def send_mixed(mixed):
        return [mixed] + [hop(mixed[at], "gene", keys[at]) for at in range(1, gene_count)]

    blocks = spread(normed, "gene")
    (mixed,) = attend(blocks, flat_within, cell_ids, in_cell, heads, head_width)
    rows = (modules, share, width)
    mid, normed = out_call(
        out_kernel,
        me,
        keys,
        send_mixed(mixed),
        out_within,
        resid,
        [shape_of(rows, F32), shape_of(rows, BF16)],
    )

    normed = stack([normed], [seen])[0]

    keep, send = attend(
        spread(normed, "gene"), flat_cross, group_ids, across, heads, head_width, out_cross
    )
    got = hop(send, "gene", straight(1))
    for key in far[::-1]:
        keep, send = halve(keep, got, dtype=F32)
        got = hop(send, "gene", key)
    hidden = pool(mid, keep, got)

    hids = spread(hidden, "gene")
    far_hids = [stack([hop(hidden, "grp", straight(rel)) for rel in range(1, grp_count)], hids)]
    far_hids += [hop(far_hids[0], "gene", key) for key in keys[1 : gene_count // 2]]
    high, low, sums, own_hid = decode(
        me, keys, counts_t, panel_col, panel_row, library / genes_all, w_mean_t, w_disp_t, hids, norm
    )
    groups = [(own_hid, high, low)]
    far_hids = [stack(far_hids, [high])]
    far_hids.append(hop(far_hids[0], "gene", straight(1)))
    for other in range(grp_count - 1):
        high, low, hid = far_call(
            place, keys, other, seen, panel_col, w_mean_t, w_disp_t, far_hids, norm, genes_all
        )
        groups.append((hid, high, low))
    bits = gene_count.bit_length() - 1
    for bit in range(bits):
        after = [groups[min(bit, grp_count - 1)][1]]
        sums = add(sums, hop(sums, "gene", straight(1 << bit)), after)
    sums = [sums] + [hop(sums, "grp", straight(rel)) for rel in range(1, grp_count)]
    grad_mean = in_hbm(grad_mean_call(place, groups))
    grad_disp, loss = disp_call(
        place, sums, [group[0] for group in groups], w_disp_t, norm, genes_all, [grad_mean]
    )
    return (loss.reshape(cells), grad_mean, grad_disp.T)


def solution(mesh):
    return jax.shard_map(
        shards,
        mesh=mesh,
        in_specs=(
            P("grp", "gene"),
            P("gene"),
            P("grp", None),
            P("gene", None),
            P(None, "gene", None),
            P("gene", None, None),
            P(None, "gene", None),
            P("gene", None, None),
            P(None, "gene"),
            P(),
        ),
        out_specs=(P("grp"), P("grp", "gene"), P()),
        check_vma=False,
    )
```

```python
import functools

import jax
import jax.numpy as jnp
from jax import lax
from jax.experimental import pallas as pl
from jax.experimental.pallas import tpu as pltpu
from jax.sharding import PartitionSpec as P

EPS = 1e-06
FLOOR = 0.3
TARGET = 10000.0
DISP_BASE = 0.5
COUNT_MOST = 12
LANES = 128
EXTRA = 16
LOG2_E = 1.4426950408889634

F32 = jnp.float32
BF16 = jnp.bfloat16
NT = (((1,), (1,)), ((), ()))
PARAMS = pltpu.CompilerParams(vmem_limit_bytes=12 * 1024 * 1024)
LARGE = pltpu.CompilerParams(vmem_limit_bytes=20 * 1024 * 1024)
WHOLE = pl.BlockSpec(memory_space=pltpu.VMEM)
SCALAR = pl.BlockSpec(memory_space=pltpu.SMEM)
ANYWHERE = pl.BlockSpec(memory_space=pl.ANY)


def in_hbm(array):
    return pltpu.with_memory_space_constraint(array, pltpu.HBM)


def shape_of(shape, dtype):
    return jax.ShapeDtypeStruct(shape, dtype)


def launch(kernel, args, in_specs, after=(), params=PARAMS, **options):
    count = len(args)

    def body(*refs):
        kernel(*refs[:count], *refs[count + len(after) :])

    return pl.pallas_call(
        body,
        in_specs=list(in_specs) + [ANYWHERE] * len(after),
        compiler_params=params,
        **options,
    )(*args, *after)


def fixed(*shape):
    return pl.BlockSpec(shape, lambda i: (0,) * len(shape))


def dot_nt(left, right):
    return lax.dot_general(left, right, NT, preferred_element_type=F32)


def dot_nn(left, right):
    return jnp.dot(left, right, preferred_element_type=F32)


def split2(value):
    high = value.astype(BF16)
    return high, (value - high.astype(F32)).astype(BF16)


def split3(value):
    high = value.astype(BF16)
    rest = value - high.astype(F32)
    middle = rest.astype(BF16)
    return high, middle, (rest - middle.astype(F32)).astype(BF16)


def softplus(value):
    return jnp.maximum(value, 0.0) + jnp.log1p(jnp.exp(-jnp.abs(value)))


def sigmoid(value):
    return 1.0 / (1.0 + jnp.exp(-value))


def rms_rows(values):
    return values * lax.rsqrt(jnp.mean(values * values, axis=-1, keepdims=True) + EPS)


def tile_of(extent, unit, most):
    for tile in range(min(most, extent) // unit * unit, 0, -unit):
        if extent % tile == 0:
            return tile
    return extent


def hop(value, axis, key):
    size = lax.axis_size(axis)
    return lax.ppermute(value, axis, [(i, i ^ key[i & 1]) for i in range(size)])


def straight(mask):
    return (mask, mask)


def far_keys(size):
    masks = [1 << bit for bit in range(1, size.bit_length() - 1)]
    return list(zip(masks, masks[::-1]))


def spread_keys(size):
    keys = [(0, 0)]
    for even, odd in far_keys(size):
        keys += [(e ^ even, o ^ odd) for e, o in keys]
    return keys + [(1 ^ o, 1 ^ e) for e, o in keys]


def spread(own, axis):
    size = lax.axis_size(axis)
    blocks = [own]
    for at, key in enumerate(far_keys(size)):
        if at:
            blocks[0] = stack([own], blocks[1:])[0]
        blocks += [hop(block, axis, key) for block in blocks]
    return blocks + [hop(block, axis, straight(1)) for block in blocks]


def holder(me, key):
    even, odd = key
    return me ^ (even + (me & 1) * (odd - even))


def project_kernel(keys, me_ref, counts_ref, scale_ref, w_ref, keep_ref, send_ref, x_ref, flat_ref):
    share = x_ref.shape[0] // len(keys)
    half = keep_ref.shape[0]

    @pl.when(pl.program_id(0) == 0)
    def _():
        scaled = jnp.log1p(counts_ref[...].astype(F32) * scale_ref[...])
        flat_ref[...] = scaled.T.astype(BF16)
        for place, key in enumerate(keys):
            x_ref[place * share : (place + 1) * share, :] = flat_ref[
                pl.ds(holder(me_ref[0], key) * share, share), :
            ]

    part = dot_nn(x_ref[...], w_ref[...])
    keep_ref[...] = part[:half]
    send_ref[...] = part[half:]


def project(me, counts_t, scale, w_proj, keys, chunk, chunks, after):
    genes, cells = counts_t.shape
    columns = w_proj.shape[1] // chunks
    tile = tile_of(columns, LANES, 640)
    steps = columns // tile
    half = cells // 2
    out = shape_of((half, columns), F32)
    return launch(
        functools.partial(project_kernel, keys),
        (me, counts_t, scale, in_hbm(w_proj)),
        [
            SCALAR,
            fixed(genes, cells),
            fixed(1, cells),
            pl.BlockSpec((genes, tile), lambda i: (0, chunk * steps + i)),
        ],
        after,
        grid=(steps,),
        out_shape=(out, out),
        out_specs=[pl.BlockSpec((half, tile), lambda i: (0, i))] * 2,
        scratch_shapes=[pltpu.VMEM((cells, genes), BF16), pltpu.VMEM((cells, genes), BF16)],
        cost_estimate=pl.CostEstimate(
            flops=2 * cells * genes * columns,
            bytes_accessed=genes * columns * 2 + cells * columns * 4,
            transcendentals=cells * genes,
        ),
    )


def halve_kernel(keep_ref, got_ref, stay_ref, go_ref):
    half = stay_ref.shape[0]
    total = keep_ref[...] + got_ref[...].astype(F32)
    stay_ref[...] = total[:half]
    go_ref[...] = total[half:].astype(go_ref.dtype)


def halve(keep, got, after=(), dtype=BF16):
    rows, *columns = keep.shape
    out = (rows // 2, *columns)
    size = keep.size
    return launch(
        halve_kernel,
        (keep, got),
        [WHOLE] * 2,
        after,
        out_shape=(shape_of(out, F32), shape_of(out, dtype)),
        out_specs=[WHOLE] * 2,
        cost_estimate=pl.CostEstimate(
            flops=size, bytes_accessed=size * 11, transcendentals=0
        ),
    )


def rows_kernel(chunks, *refs):
    tokens_ref, normed_ref = refs[2 * chunks :]
    width = tokens_ref.shape[2]
    parts = tokens_ref.shape[0] // chunks
    for chunk in range(chunks):
        total = refs[2 * chunk][...] + refs[2 * chunk + 1][...].astype(F32)
        for at in range(parts):
            rows = total[:, at * width : (at + 1) * width]
            tokens_ref[chunk * parts + at] = rows
            normed_ref[chunk * parts + at] = rms_rows(rows).astype(BF16)


def to_rows(pairs, width):
    share, columns = pairs[0][0].shape
    shape = (len(pairs) * columns // width, share, width)
    return launch(
        functools.partial(rows_kernel, len(pairs)),
        [part for pair in pairs for part in pair],
        [WHOLE] * 2 * len(pairs),
        out_shape=(shape_of(shape, F32), shape_of(shape, BF16)),
        out_specs=[WHOLE] * 2,
        cost_estimate=pl.CostEstimate(
            flops=12 * share * columns, bytes_accessed=share * columns * 24, transcendentals=0
        ),
    )


def attend_kernel(pieces, heads, head_width, outs, w_ref, row_ref, col_ref, *refs):
    blocks = refs[: -4 - outs]
    out_refs, refs = refs[-4 - outs : -4], refs[-4:]
    x_ref, query_ref, keys_ref, values_ref = refs
    if outs == 2:
        blocks, blocks_out = blocks[:-1], blocks[-1]
    used = heads * head_width
    _, share, _ = blocks[0].shape
    rows = len(pieces[0]) * share
    places = [spot for piece in pieces for spot in piece]
    for at, (block, module) in enumerate(places):
        x_ref[at * share : (at + 1) * share, :] = blocks[block][module]
    lane = lax.broadcasted_iota(jnp.int32, (1, used), 1)
    picks = [(lax.rem(lane, heads) == h).astype(F32).astype(BF16) for h in range(heads)]
    down = lax.rem(lax.broadcasted_iota(jnp.int32, (used, used), 0), heads)
    over = lax.rem(lax.broadcasted_iota(jnp.int32, (used, used), 1), heads)
    same_head = (down == over).astype(F32).astype(BF16)

    def head_norm(values):
        high, low = split2(values * values)
        mean = (dot_nn(high, same_head) + dot_nn(low, same_head)) * (1.0 / head_width)
        return (values * lax.rsqrt(jnp.maximum(mean, FLOOR))).astype(BF16)

    every = x_ref.shape[0]
    step = min(every, 256)
    for at in range(0, every, step):
        part = slice(at, at + step)
        qkv = dot_nt(x_ref[part, :], w_ref[...])
        query_ref[part, :] = head_norm(qkv[:, :used])
        keys_ref[part, :] = head_norm(qkv[:, used : 2 * used])
        values_ref[part, :] = qkv[:, 2 * used :].astype(BF16)
    same = row_ref[...] == col_ref[...]
    scale = head_width ** (-0.5) * LOG2_E
    summed = None
    for at, piece in enumerate(pieces):
        part = slice(at * rows, (at + 1) * rows)
        query, keys, values = query_ref[part, :], keys_ref[part, :], values_ref[part, :]
        mixed = jnp.zeros((rows, used), F32)
        for pick in picks:
            weights = jnp.where(same, jnp.exp2(dot_nt(query * pick, keys) * scale), 0.0)
            probs = weights * (1.0 / jnp.sum(weights, axis=-1, keepdims=True))
            mixed = mixed + dot_nn(probs.astype(BF16), values * pick)
        mixed = mixed.astype(BF16)
        if outs == 1:
            for place, (block, module) in enumerate(piece):
                out_refs[0][block, module * share : (module + 1) * share, :] = mixed[
                    place * share : (place + 1) * share
                ]
        else:
            mixed = mixed.astype(F32)
            summed = mixed if summed is None else summed + mixed
    if outs == 2:
        w_out = blocks_out[...]
        high, middle, low = split3(summed * (1.0 / len(pieces)))
        total = dot_nn(high, w_out) + dot_nn(middle, w_out) + dot_nn(low, w_out)
        for at in range(rows // share):
            half = rows // share // 2
            out_refs[at // half][at % half] = total[at * share : (at + 1) * share]


def attend(blocks, w_flat, ids, pieces, heads, head_width, w_out=None, after=()):
    count = len(blocks)
    modules, share, width = blocks[0].shape
    rows = len(pieces[0]) * share
    every = len(pieces) * rows
    used = heads * head_width
    if w_out is None:
        last, out_shape = [], [shape_of((count, modules * share, used), BF16)]
    else:
        last, out_shape = [w_out], [shape_of((count // 2, share, width), F32)] * 2
    return launch(
        functools.partial(attend_kernel, pieces, heads, head_width, len(out_shape)),
        (w_flat, *ids, *blocks, *last),
        [WHOLE] * (3 + len(blocks) + len(last)),
        after,
        out_shape=out_shape,
        out_specs=[WHOLE] * len(out_shape),
        scratch_shapes=[pltpu.VMEM((every, width), BF16)] + [pltpu.VMEM((every, used), BF16)] * 3,
        cost_estimate=pl.CostEstimate(
            flops=2 * every * (width * 3 * used + 2 * heads * rows * used),
            bytes_accessed=every * width * 2 + 3 * used * width * 2 + every * used * 2,
            transcendentals=every * rows * heads,
        ),
    )


def add_mixed(places, keys, me_ref, w_hbm, resid_hbm, mixed_hbm, scratch):
    mixed_ref, w_ref, resid_ref, sems = scratch
    modules, share, _ = resid_ref.shape
    count = len(keys)
    copies = []
    for at, (place, key) in enumerate(zip(places, keys)):
        source = mixed_hbm[0].at[0] if place == 0 else mixed_hbm[place]
        pair = [
            pltpu.make_async_copy(source, mixed_ref.at[at], sems.at[2 * at]),
            pltpu.make_async_copy(
                w_hbm.at[holder(me_ref[0], key)], w_ref.at[at], sems.at[2 * at + 1]
            ),
        ]
        for copy in pair:
            copy.start()
        copies.append(pair)
    resid_copy = pltpu.make_async_copy(resid_hbm, resid_ref, sems.at[2 * count])
    resid_copy.start()
    total = None
    for at, pair in enumerate(copies):
        for copy in pair:
            copy.wait()
        term = dot_nn(mixed_ref[at], w_ref[at])
        total = term if total is None else total + term
    resid_copy.wait()
    return [resid_ref[m] + total[m * share : (m + 1) * share] for m in range(modules)]


def out_kernel(places, keys, me_ref, w_hbm, resid_hbm, *refs):
    mixed, (mid_ref, normed_ref), scratch = refs[:-6], refs[-6:-4], refs[-4:]
    modules = add_mixed(places, keys, me_ref, w_hbm, resid_hbm, mixed, scratch)
    for m, rows in enumerate(modules):
        mid_ref[m] = rows
        normed_ref[m] = rms_rows(rows).astype(BF16)


def add_split_kernel(keep_ref, got_ref, *out_refs):
    for at, out_ref in enumerate(out_refs):
        out_ref[...] = keep_ref[at] + got_ref[at]


def add_split(keep, got):
    count, *rest = keep.shape
    return launch(
        add_split_kernel,
        (keep, got),
        [WHOLE] * 2,
        out_shape=[shape_of(tuple(rest), F32)] * count,
        out_specs=[WHOLE] * count,
    )


def pool_kernel(resid_ref, *refs):
    modules = resid_ref.shape[0]
    total = functools.reduce(jnp.add, [resid_ref[m] for m in range(modules)])
    parts = functools.reduce(jnp.add, [ref[...] for ref in refs[:-1]])
    refs[-1][...] = rms_rows(total * (1.0 / modules) + parts).astype(BF16)


def pool(resid, parts):
    return launch(
        pool_kernel,
        (resid, *parts),
        [WHOLE] * (1 + len(parts)),
        out_shape=shape_of(parts[0].shape, BF16),
        out_specs=WHOLE,
    )


def out_call(kernel, me, keys, mixed, w_all, resid, out_shape, after=()):
    back = [(o, e) if e & 1 else (e, o) for e, o in keys]
    _, rows, inner = mixed[0].shape
    width = w_all.shape[-1]
    count = len(keys)
    return launch(
        functools.partial(kernel, [back.index(key) for key in keys], keys),
        (me, in_hbm(w_all), resid, *mixed),
        [SCALAR, ANYWHERE, ANYWHERE] + [ANYWHERE] * len(mixed),
        after,
        out_shape=out_shape,
        out_specs=[WHOLE] * len(out_shape),
        scratch_shapes=[
            pltpu.VMEM((count, rows, inner), BF16),
            pltpu.VMEM(w_all.shape, BF16),
            pltpu.VMEM(resid.shape, F32),
            pltpu.SemaphoreType.DMA((2 * count + 1,)),
        ],
        cost_estimate=pl.CostEstimate(
            flops=2 * rows * count * inner * width,
            bytes_accessed=count * inner * (width + rows) * 2 + rows * width * 10,
            transcendentals=0,
        ),
    )


def panel_table(w_disp_ref, hidden, with_log):
    base = DISP_BASE + softplus(dot_nt(w_disp_ref[...], hidden))
    parts = split3(base)
    if with_log:
        parts = [jnp.concatenate(pair, axis=1) for pair in zip(parts, split3(jnp.log(base)))]
    return jnp.concatenate([p.astype(F32) for p in parts], axis=0).astype(BF16)


def panel_pick(panel_ref, panel_count):
    genes = panel_ref.shape[0]
    over = lax.rem(lax.broadcasted_iota(jnp.int32, (genes, 3 * panel_count), 1), panel_count)
    return (panel_ref[...] == over).astype(F32).astype(BF16)


def place_cells(keys, me, blocks, hid_ref):
    share = blocks[0].shape[0]
    for key, block in zip(keys, blocks):
        hid_ref[pl.ds(holder(me, key) * share, share), :] = block


def rate_terms(logit, rate_scale, theta, seen, norm):
    small = jnp.exp(-jnp.abs(logit))
    soft = jnp.maximum(logit, 0.0) + jnp.log1p(small)
    rate = rate_scale * soft
    total = theta + rate
    above = theta * (rate - seen) * jnp.where(logit >= 0.0, norm, norm * small)
    d_logit = above / (soft * total * (1.0 + small))
    return rate, total, d_logit


def decode_kernel(
    keys, norm, me_ref, counts_ref, col_ref, row_ref, scale_ref, wm_ref, wd_ref, *refs
):
    hids = refs[: len(keys)]
    high_ref, low_ref, sum_ref, hid_ref, table_ref = refs[len(keys) :]
    cells = hid_ref.shape[0]
    panel_count = wd_ref.shape[0]

    @pl.when(pl.program_id(0) == 0)
    def _():
        place_cells(keys, me_ref[0], [block[...] for block in hids], hid_ref)
        table_ref[...] = panel_table(wd_ref, hid_ref[...], True)
        sum_ref[...] = jnp.zeros_like(sum_ref)

    both = dot_nn(panel_pick(col_ref, panel_count), table_ref[...])
    theta, log_theta = both[:, :cells], both[:, cells:]
    seen = counts_ref[...].astype(F32)
    rate, total, d_logit = rate_terms(
        dot_nt(wm_ref[...], hid_ref[...]), scale_ref[...], theta, seen, norm
    )
    high_ref[...], low_ref[...] = split2(d_logit)
    log_total = jnp.log(total)
    product = jnp.ones_like(theta)
    slope = jnp.zeros_like(theta)
    for k in range(COUNT_MOST):
        inverse = 1.0 / (k + 1.0)
        factor = theta * inverse + k * inverse
        here = seen > k
        slope = jnp.where(here, slope * factor + product * inverse, slope)
        product = jnp.where(here, product * factor, product)
    nll = -(
        jnp.log(product)
        + theta * (log_theta - log_total)
        + seen * (jnp.log(rate) - log_total)
    )
    d_theta = -(slope / product + log_theta + 1.0 - log_total - (theta + seen) / total)
    down = lax.broadcasted_iota(jnp.int32, (panel_count, theta.shape[0]), 0)
    pick = (down == row_ref[0]).astype(F32).astype(BF16)
    high, middle, low = split3(d_theta)
    sum_ref[:panel_count, :] += dot_nn(pick, high) + dot_nn(pick, middle) + dot_nn(pick, low)
    sum_ref[panel_count : panel_count + 1, :] += jnp.sum(nll, axis=0, keepdims=True)


def decode(me, keys, counts_t, panel_col, panel_row, rate_scale, w_mean_t, w_disp_t, hids, norm):
    genes, cells = counts_t.shape
    width = w_mean_t.shape[1]
    panel_count = w_disp_t.shape[0]
    steps, _, tile = panel_row.shape
    wide = -(-(panel_count + 1) // 8) * 8
    by_gene = lambda columns: pl.BlockSpec((tile, columns), lambda i: (i, 0))
    return launch(
        functools.partial(decode_kernel, keys, norm),
        (
            me,
            counts_t,
            panel_col,
            panel_row,
            rate_scale,
            in_hbm(w_mean_t),
            w_disp_t,
            *hids,
        ),
        [
            SCALAR,
            by_gene(cells),
            by_gene(1),
            pl.BlockSpec((1, 1, tile), lambda i: (i, 0, 0)),
            fixed(1, cells),
            by_gene(width),
            fixed(panel_count, width),
        ]
        + [fixed(*hids[0].shape)] * len(hids),
        grid=(steps,),
        out_shape=(
            shape_of((genes, cells), BF16),
            shape_of((genes, cells), BF16),
            shape_of((wide, cells), F32),
            shape_of((cells, width), BF16),
        ),
        out_specs=[by_gene(cells), by_gene(cells), fixed(wide, cells), fixed(cells, width)],
        scratch_shapes=[pltpu.VMEM((3 * panel_count, 2 * cells), BF16)],
        cost_estimate=pl.CostEstimate(
            flops=2 * genes * cells * width + 150 * genes * cells,
            bytes_accessed=genes * (width * 2 + cells * 8),
            transcendentals=8 * genes * cells,
        ),
    )


def far_kernel(keys, norm, genes_all, place_ref, seen_ref, lib_ref, col_ref, wm_ref, wd_ref, *refs):
    hids = refs[:2]
    high_ref, low_ref, hid_ref, table_ref = refs[2:]
    seen = seen_ref[0].astype(F32)
    lib = lib_ref[0].astype(F32)
    panel_count = wd_ref.shape[0]

    @pl.when(pl.program_id(0) == 0)
    def _():
        blocks = [half[at, 0] for half in hids for at in range(half.shape[0])]
        place_cells(keys, place_ref[0], blocks, hid_ref)
        table_ref[...] = panel_table(wd_ref, hid_ref[...], False)

    library = jnp.sum(lib, axis=0, keepdims=True)
    _, _, d_logit = rate_terms(
        dot_nt(wm_ref[...], hid_ref[...]),
        library / genes_all,
        dot_nn(panel_pick(col_ref, panel_count), table_ref[...]),
        seen,
        norm,
    )
    high_ref[...], low_ref[...] = split2(d_logit)


def far_call(place, keys, other, seen, panel_col, w_mean_t, w_disp_t, hids, norm, genes_all):
    genes, width = w_mean_t.shape
    cells = seen.shape[2]
    panel_count = w_disp_t.shape[0]
    near, _, share, _ = hids[0].shape
    tile = tile_of(genes, 16, 256)
    by_gene = lambda columns: pl.BlockSpec((tile, columns), lambda i, at: (i, 0))
    last = genes // EXTRA
    return pl.pallas_call(
        functools.partial(far_kernel, keys, norm, genes_all),
        grid_spec=pltpu.PrefetchScalarGridSpec(
            num_scalar_prefetch=1,
            grid=(genes // tile,),
            in_specs=[
                pl.BlockSpec((1, tile, cells), lambda i, at: (at[1] ^ other, i, 0)),
                pl.BlockSpec((1, EXTRA, cells), lambda i, at: (at[1] ^ other, last, 0)),
                by_gene(1),
                by_gene(width),
                pl.BlockSpec((panel_count, width), lambda i, at: (0, 0)),
            ]
            + [pl.BlockSpec((near, 1, share, width), lambda i, at: (0, other - 1, 0, 0))]
            * len(hids),
            out_specs=[
                by_gene(cells),
                by_gene(cells),
                pl.BlockSpec((cells, width), lambda i, at: (0, 0)),
            ],
            scratch_shapes=[pltpu.VMEM((3 * panel_count, cells), BF16)],
        ),
        out_shape=(
            shape_of((genes, cells), BF16),
            shape_of((genes, cells), BF16),
            shape_of((cells, width), BF16),
        ),
        compiler_params=PARAMS,
        cost_estimate=pl.CostEstimate(
            flops=2 * genes * cells * width + 60 * genes * cells,
            bytes_accessed=genes * (width * 2 + cells * 6),
            transcendentals=4 * genes * cells,
        ),
    )(place, seen, seen, panel_col, in_hbm(w_mean_t), w_disp_t, *hids)


def grad_kernel(place_ref, *refs):
    out_ref = refs[-1]
    mine, width = out_ref.shape[0], refs[0].shape[1]
    down = lax.broadcasted_iota(jnp.int32, (mine, width), 0) + place_ref[1] * mine
    over = lax.broadcasted_iota(jnp.int32, (mine, width), 1)
    pick = (down == over).astype(F32).astype(BF16)
    total = None
    for at in range(0, len(refs) - 1, 3):
        hidden = dot_nt(pick, refs[at][...]).astype(BF16)
        term = dot_nt(hidden, refs[at + 1][...]) + dot_nt(hidden, refs[at + 2][...])
        total = term if total is None else total + term
    out_ref[...] = total


def grad_mean_call(place, groups):
    cells, width = groups[0][0].shape
    genes = groups[0][1].shape[0]
    mine = width // len(groups)
    return launch(
        grad_kernel,
        (place, *[array for group in groups for array in group]),
        [SCALAR] + [WHOLE] * 3 * len(groups),
        params=LARGE,
        out_shape=shape_of((mine, genes), F32),
        out_specs=WHOLE,
        cost_estimate=pl.CostEstimate(
            flops=2 * len(groups) * cells * mine * (width + 2 * genes),
            bytes_accessed=len(groups) * cells * (width + 2 * genes) * 2 + mine * genes * 4,
            transcendentals=0,
        ),
    )


def disp_kernel(norm, genes_all, place_ref, wd_ref, *refs):
    count = (len(refs) - 3) // 2
    sums, hids = refs[:count], refs[count : 2 * count]
    grad_ref, loss_ref, term_ref = refs[2 * count :]
    panel_count = wd_ref.shape[0]
    for other in range(count):
        hidden = hids[other][...]
        d_disp = sums[other][:panel_count] * sigmoid(dot_nt(wd_ref[...], hidden)) * norm
        parts = jnp.concatenate([part.astype(F32) for part in split3(d_disp)], axis=0)
        three = dot_nn(parts.astype(BF16), hidden)
        term_ref[place_ref[1] ^ other] = (
            three[:panel_count]
            + three[panel_count : 2 * panel_count]
            + three[2 * panel_count :]
        )
    total = term_ref[0]
    for block in range(1, count):
        total = total + term_ref[block]
    grad_ref[...] = total
    loss_ref[...] = sums[0][panel_count : panel_count + 1] * (1.0 / genes_all)


def disp_call(place, sums, hids, w_disp_t, norm, genes_all, after):
    panel_count, width = w_disp_t.shape
    cells = sums[0].shape[1]
    return launch(
        functools.partial(disp_kernel, norm, genes_all),
        (place, w_disp_t, *sums, *hids),
        [SCALAR] + [WHOLE] * (1 + len(sums) + len(hids)),
        after,
        out_shape=(shape_of((panel_count, width), F32), shape_of((1, cells), F32)),
        out_specs=[WHOLE] * 2,
        scratch_shapes=[pltpu.VMEM((len(sums), panel_count, width), F32)],
    )


def pack_kernel(counts_ref, library_ref, out_ref):
    genes, cells = counts_ref.shape
    out_ref[:genes, :] = counts_ref[...].astype(F32).astype(BF16)
    parts = [part.astype(F32) for part in split3(library_ref[...])]
    parts.append(jnp.zeros((EXTRA - len(parts), cells), F32))
    out_ref[genes:, :] = jnp.concatenate(parts, axis=0).astype(BF16)


def pack(counts_t, library, after):
    genes, cells = counts_t.shape
    return launch(
        pack_kernel,
        (counts_t, library),
        [WHOLE] * 2,
        after,
        out_shape=shape_of((genes + EXTRA, cells), BF16),
        out_specs=WHOLE,
    )


def add_kernel(left_ref, right_ref, out_ref):
    out_ref[...] = left_ref[...] + right_ref[...]


def add(left, right, after):
    return launch(
        add_kernel,
        (left, right),
        [WHOLE] * 2,
        after,
        out_shape=shape_of(left.shape, left.dtype),
        out_specs=WHOLE,
    )


def stack_kernel(*refs):
    for at, ref in enumerate(refs[:-1]):
        refs[-1][at] = ref[...]


def stack(parts, after):
    return launch(
        stack_kernel,
        parts,
        [WHOLE] * len(parts),
        after,
        out_shape=shape_of((len(parts),) + parts[0].shape, parts[0].dtype),
        out_specs=WHOLE,
    )


def flat_qkv(weights):
    return weights.transpose(2, 1, 0).reshape(-1, weights.shape[0])


def flat_out(weights):
    return weights.transpose(1, 0, 2).reshape(-1, weights.shape[2])


def shards(
    counts,
    panels,
    membership,
    w_proj,
    w_qkv_within,
    w_out_within,
    w_qkv_cross,
    w_out_cross,
    w_mean,
    w_disp,
):
    cells, genes_here = counts.shape
    width, heads, triple = w_qkv_within.shape
    head_width = triple // 3
    modules = w_proj.shape[1] // width
    gene_count = lax.axis_size("gene")
    grp_count = lax.axis_size("grp")
    genes_all = genes_here * gene_count
    share = cells // gene_count
    panel_count = w_disp.shape[1]
    norm = float(cells * grp_count) ** (-0.5)
    gene_me = lax.axis_index("gene").astype(jnp.int32)
    grp_me = lax.axis_index("grp").astype(jnp.int32)
    me = gene_me.reshape(1)
    place = jnp.stack([gene_me, grp_me])
    keys = spread_keys(gene_count)
    far = far_keys(gene_count)

    counts_t = counts.T
    w_mean_t = w_mean.T
    w_disp_t = w_disp.T

    library = jnp.sum(counts_t.astype(F32), axis=0, keepdims=True)
    for bit in range(gene_count.bit_length() - 1):
        library = library + hop(library, "gene", straight(1 << bit))
    library = 1.0 + library
    flat_within = flat_qkv(w_qkv_within)
    flat_cross = flat_qkv(w_qkv_cross)
    out_within = in_hbm(lax.all_gather(flat_out(w_out_within), "gene"))
    out_cross = flat_out(w_out_cross)
    cell_ids = jnp.tile(jnp.arange(share, dtype=jnp.int32), modules)
    odd = (gene_me & 1) == 1
    owners = gene_me ^ jnp.where(odd, jnp.array([o for _, o in keys]), jnp.array([e for e, _ in keys]))
    group_ids = jnp.take(membership.reshape(gene_count, share), owners, axis=0).reshape(-1)
    cell_ids = (cell_ids.reshape(-1, 1), cell_ids.reshape(1, -1))
    group_ids = (group_ids.reshape(-1, 1), group_ids.reshape(1, -1))
    tile = tile_of(genes_here, 16, 256)
    panel_col = panels.reshape(genes_here, 1)
    panel_row = panels.reshape(genes_here // tile, 1, tile)

    halves = []
    early = [*cell_ids, *group_ids, panel_col, panel_row]
    for chunk in range(2):
        keep, send = project(me, counts_t, TARGET / library, w_proj, keys, chunk, 2, early)
        early = []
        halves.append((keep, hop(send, "gene", straight(1))))
    laid = [[flat_within], [flat_cross, out_cross]]
    for at, key in enumerate(far[::-1]):
        nexts = []
        for chunk, (keep, got) in enumerate(halves):
            keep, send = halve(keep, got, laid[chunk] if at == 1 else ())
            nexts.append((keep, hop(send, "gene", key)))
        halves = nexts
    resid, normed = to_rows(halves, width)

    packed = pack(counts_t, library, [resid])
    seen = in_hbm(lax.all_gather(packed, "grp"))
    normed = stack([normed], [out_within, packed])[0]

    in_cell = [[(block, m) for m in range(modules)] for block in range(gene_count)]
    across = [[(block, m) for block in range(gene_count)] for m in range(modules)]

    def send_mixed(mixed):
        return [mixed] + [hop(mixed[at], "gene", keys[at]) for at in range(1, gene_count)]

    blocks = spread(normed, "gene")
    (mixed,) = attend(blocks, flat_within, cell_ids, in_cell, heads, head_width)
    rows = (modules, share, width)
    mid, normed = out_call(
        out_kernel,
        me,
        keys,
        send_mixed(mixed),
        out_within,
        resid,
        [shape_of(rows, F32), shape_of(rows, BF16)],
    )

    normed = stack([normed], [seen])[0]

    keep, send = attend(
        spread(normed, "gene"), flat_cross, group_ids, across, heads, head_width, out_cross
    )
    got = hop(send, "gene", straight(1))
    parts = list(add_split(keep, got))
    parts = parts[:1] + [hop(part, "gene", key) for part, key in zip(parts[1:], keys[1:])]
    hidden = pool(mid, parts)

    hids = [hidden] + [hop(hidden, "gene", key) for key in keys[1 : gene_count // 2]]
    hids += [hop(block, "gene", straight(1)) for block in hids]
    far_hids = [stack([hop(hidden, "grp", straight(rel)) for rel in range(1, grp_count)], hids)]
    far_hids += [hop(far_hids[0], "gene", key) for key in keys[1 : gene_count // 2]]
    high, low, sums, own_hid = decode(
        me, keys, counts_t, panel_col, panel_row, library / genes_all, w_mean_t, w_disp_t, hids, norm
    )
    groups = [(own_hid, high, low)]
    far_hids = [stack(far_hids, [high])]
    far_hids.append(hop(far_hids[0], "gene", straight(1)))
    for other in range(1, grp_count):
        high, low, hid = far_call(
            place, keys, other, seen, panel_col, w_mean_t, w_disp_t, far_hids, norm, genes_all
        )
        groups.append((hid, high, low))
    bits = gene_count.bit_length() - 1
    for bit in range(bits):
        after = [groups[min(bit, grp_count - 1)][1]]
        sums = add(sums, hop(sums, "gene", straight(1 << bit)), after)
    sums = [sums] + [hop(sums, "grp", straight(rel)) for rel in range(1, grp_count)]
    grad_mean = in_hbm(grad_mean_call(place, groups))
    grad_disp, loss = disp_call(
        place, sums, [group[0] for group in groups], w_disp_t, norm, genes_all, [grad_mean]
    )
    return (loss.reshape(cells), grad_mean, grad_disp.T)


def solution(mesh):
    return jax.shard_map(
        shards,
        mesh=mesh,
        in_specs=(
            P("grp", "gene"),
            P("gene"),
            P("grp", None),
            P("gene", None),
            P(None, "gene", None),
            P("gene", None, None),
            P(None, "gene", None),
            P("gene", None, None),
            P(None, "gene"),
            P(),
        ),
        out_specs=(P("grp"), P("grp", "gene"), P()),
        check_vma=False,
    )
```

```python
import functools

import jax
import jax.numpy as jnp
from jax import lax
from jax.experimental import pallas as pl
from jax.experimental.pallas import tpu as pltpu
from jax.sharding import PartitionSpec as P

EPS = 1e-06
FLOOR = 0.3
TARGET = 10000.0
DISP_BASE = 0.5
COUNT_MOST = 12
LANES = 128
EXTRA = 16
LOG2_E = 1.4426950408889634

F32 = jnp.float32
BF16 = jnp.bfloat16
NT = (((1,), (1,)), ((), ()))
PARAMS = pltpu.CompilerParams(vmem_limit_bytes=12 * 1024 * 1024)
LARGE = pltpu.CompilerParams(vmem_limit_bytes=20 * 1024 * 1024)
WHOLE = pl.BlockSpec(memory_space=pltpu.VMEM)
SCALAR = pl.BlockSpec(memory_space=pltpu.SMEM)
ANYWHERE = pl.BlockSpec(memory_space=pl.ANY)


def in_hbm(array):
    return pltpu.with_memory_space_constraint(array, pltpu.HBM)


def shape_of(shape, dtype):
    return jax.ShapeDtypeStruct(shape, dtype)


def launch(kernel, args, in_specs, after=(), params=PARAMS, **options):
    count = len(args)

    def body(*refs):
        kernel(*refs[:count], *refs[count + len(after) :])

    return pl.pallas_call(
        body,
        in_specs=list(in_specs) + [ANYWHERE] * len(after),
        compiler_params=params,
        **options,
    )(*args, *after)


def fixed(*shape):
    return pl.BlockSpec(shape, lambda i: (0,) * len(shape))


def dot_nt(left, right):
    return lax.dot_general(left, right, NT, preferred_element_type=F32)


def dot_nn(left, right):
    return jnp.dot(left, right, preferred_element_type=F32)


def split2(value):
    high = value.astype(BF16)
    return high, (value - high.astype(F32)).astype(BF16)


def split3(value):
    high = value.astype(BF16)
    rest = value - high.astype(F32)
    middle = rest.astype(BF16)
    return high, middle, (rest - middle.astype(F32)).astype(BF16)


def softplus(value):
    return jnp.maximum(value, 0.0) + jnp.log1p(jnp.exp(-jnp.abs(value)))


def sigmoid(value):
    return 1.0 / (1.0 + jnp.exp(-value))


def rms_rows(values):
    return values * lax.rsqrt(jnp.mean(values * values, axis=-1, keepdims=True) + EPS)


def tile_of(extent, unit, most):
    for tile in range(min(most, extent) // unit * unit, 0, -unit):
        if extent % tile == 0:
            return tile
    return extent


def hop(value, axis, key):
    size = lax.axis_size(axis)
    return lax.ppermute(value, axis, [(i, i ^ key[i & 1]) for i in range(size)])


def straight(mask):
    return (mask, mask)


def far_keys(size):
    masks = [1 << bit for bit in range(1, size.bit_length() - 1)]
    return list(zip(masks, masks[::-1]))


def spread_keys(size):
    keys = [(0, 0)]
    for even, odd in far_keys(size):
        keys += [(e ^ even, o ^ odd) for e, o in keys]
    return keys + [(1 ^ o, 1 ^ e) for e, o in keys]


def spread(own, axis):
    size = lax.axis_size(axis)
    blocks = [own]
    for at, key in enumerate(far_keys(size)):
        if at:
            blocks[0] = stack([own], blocks[1:])[0]
        blocks += [hop(block, axis, key) for block in blocks]
    return blocks + [hop(block, axis, straight(1)) for block in blocks]


def holder(me, key):
    even, odd = key
    return me ^ (even + (me & 1) * (odd - even))


def project_kernel(keys, me_ref, counts_ref, scale_ref, w_ref, keep_ref, send_ref, x_ref, flat_ref):
    share = x_ref.shape[0] // len(keys)
    half = keep_ref.shape[0]

    @pl.when(pl.program_id(0) == 0)
    def _():
        scaled = jnp.log1p(counts_ref[...].astype(F32) * scale_ref[...])
        flat_ref[...] = scaled.T.astype(BF16)
        for place, key in enumerate(keys):
            x_ref[place * share : (place + 1) * share, :] = flat_ref[
                pl.ds(holder(me_ref[0], key) * share, share), :
            ]

    part = dot_nn(x_ref[...], w_ref[...])
    keep_ref[...] = part[:half]
    send_ref[...] = part[half:]


def project(me, counts_t, scale, w_proj, keys, chunk, chunks, after):
    genes, cells = counts_t.shape
    columns = w_proj.shape[1] // chunks
    tile = tile_of(columns, LANES, 640)
    steps = columns // tile
    half = cells // 2
    out = shape_of((half, columns), F32)
    return launch(
        functools.partial(project_kernel, keys),
        (me, counts_t, scale, in_hbm(w_proj)),
        [
            SCALAR,
            fixed(genes, cells),
            fixed(1, cells),
            pl.BlockSpec((genes, tile), lambda i: (0, chunk * steps + i)),
        ],
        after,
        grid=(steps,),
        out_shape=(out, out),
        out_specs=[pl.BlockSpec((half, tile), lambda i: (0, i))] * 2,
        scratch_shapes=[pltpu.VMEM((cells, genes), BF16), pltpu.VMEM((cells, genes), BF16)],
        cost_estimate=pl.CostEstimate(
            flops=2 * cells * genes * columns,
            bytes_accessed=genes * columns * 2 + cells * columns * 4,
            transcendentals=cells * genes,
        ),
    )


def halve_kernel(keep_ref, got_ref, stay_ref, go_ref):
    half = stay_ref.shape[0]
    total = keep_ref[...] + got_ref[...].astype(F32)
    stay_ref[...] = total[:half]
    go_ref[...] = total[half:].astype(go_ref.dtype)


def halve(keep, got, after=(), dtype=BF16):
    rows, *columns = keep.shape
    out = (rows // 2, *columns)
    size = keep.size
    return launch(
        halve_kernel,
        (keep, got),
        [WHOLE] * 2,
        after,
        out_shape=(shape_of(out, F32), shape_of(out, dtype)),
        out_specs=[WHOLE] * 2,
        cost_estimate=pl.CostEstimate(
            flops=size, bytes_accessed=size * 11, transcendentals=0
        ),
    )


def rows_kernel(chunks, *refs):
    tokens_ref, normed_ref = refs[2 * chunks :]
    width = tokens_ref.shape[2]
    parts = tokens_ref.shape[0] // chunks
    for chunk in range(chunks):
        total = refs[2 * chunk][...] + refs[2 * chunk + 1][...].astype(F32)
        for at in range(parts):
            rows = total[:, at * width : (at + 1) * width]
            tokens_ref[chunk * parts + at] = rows
            normed_ref[chunk * parts + at] = rms_rows(rows).astype(BF16)


def to_rows(pairs, width):
    share, columns = pairs[0][0].shape
    shape = (len(pairs) * columns // width, share, width)
    return launch(
        functools.partial(rows_kernel, len(pairs)),
        [part for pair in pairs for part in pair],
        [WHOLE] * 2 * len(pairs),
        out_shape=(shape_of(shape, F32), shape_of(shape, BF16)),
        out_specs=[WHOLE] * 2,
        cost_estimate=pl.CostEstimate(
            flops=12 * share * columns, bytes_accessed=share * columns * 24, transcendentals=0
        ),
    )


def attend_kernel(pieces, heads, head_width, outs, w_ref, row_ref, col_ref, *refs):
    blocks = refs[: -4 - outs]
    out_refs, refs = refs[-4 - outs : -4], refs[-4:]
    x_ref, query_ref, keys_ref, values_ref = refs
    if outs == 2:
        blocks, blocks_out = blocks[:-1], blocks[-1]
    used = heads * head_width
    _, share, _ = blocks[0].shape
    rows = len(pieces[0]) * share
    places = [spot for piece in pieces for spot in piece]
    for at, (block, module) in enumerate(places):
        x_ref[at * share : (at + 1) * share, :] = blocks[block][module]
    lane = lax.broadcasted_iota(jnp.int32, (1, used), 1)
    picks = [(lax.rem(lane, heads) == h).astype(F32).astype(BF16) for h in range(heads)]
    down = lax.rem(lax.broadcasted_iota(jnp.int32, (used, used), 0), heads)
    over = lax.rem(lax.broadcasted_iota(jnp.int32, (used, used), 1), heads)
    same_head = (down == over).astype(F32).astype(BF16)

    def head_norm(values):
        high, low = split2(values * values)
        mean = (dot_nn(high, same_head) + dot_nn(low, same_head)) * (1.0 / head_width)
        return (values * lax.rsqrt(jnp.maximum(mean, FLOOR))).astype(BF16)

    every = x_ref.shape[0]
    step = min(every, 256)
    for at in range(0, every, step):
        part = slice(at, at + step)
        qkv = dot_nt(x_ref[part, :], w_ref[...])
        query_ref[part, :] = head_norm(qkv[:, :used])
        keys_ref[part, :] = head_norm(qkv[:, used : 2 * used])
        values_ref[part, :] = qkv[:, 2 * used :].astype(BF16)
    same = row_ref[...] == col_ref[...]
    scale = head_width ** (-0.5) * LOG2_E
    summed = None
    for at, piece in enumerate(pieces):
        part = slice(at * rows, (at + 1) * rows)
        query, keys, values = query_ref[part, :], keys_ref[part, :], values_ref[part, :]
        mixed = jnp.zeros((rows, used), F32)
        for pick in picks:
            weights = jnp.where(same, jnp.exp2(dot_nt(query * pick, keys) * scale), 0.0)
            probs = weights * (1.0 / jnp.sum(weights, axis=-1, keepdims=True))
            mixed = mixed + dot_nn(probs.astype(BF16), values * pick)
        mixed = mixed.astype(BF16)
        if outs == 1:
            for place, (block, module) in enumerate(piece):
                out_refs[0][block, module * share : (module + 1) * share, :] = mixed[
                    place * share : (place + 1) * share
                ]
        else:
            mixed = mixed.astype(F32)
            summed = mixed if summed is None else summed + mixed
    if outs == 2:
        w_out = blocks_out[...]
        high, middle, low = split3(summed * (1.0 / len(pieces)))
        total = dot_nn(high, w_out) + dot_nn(middle, w_out) + dot_nn(low, w_out)
        for at in range(rows // share):
            half = rows // share // 2
            out_refs[at // half][at % half] = total[at * share : (at + 1) * share]


def attend(blocks, w_flat, ids, pieces, heads, head_width, w_out=None, after=()):
    count = len(blocks)
    modules, share, width = blocks[0].shape
    rows = len(pieces[0]) * share
    every = len(pieces) * rows
    used = heads * head_width
    if w_out is None:
        last, out_shape = [], [shape_of((count, modules * share, used), BF16)]
    else:
        last, out_shape = [w_out], [shape_of((count // 2, share, width), F32)] * 2
    return launch(
        functools.partial(attend_kernel, pieces, heads, head_width, len(out_shape)),
        (w_flat, *ids, *blocks, *last),
        [WHOLE] * (3 + len(blocks) + len(last)),
        after,
        out_shape=out_shape,
        out_specs=[WHOLE] * len(out_shape),
        scratch_shapes=[pltpu.VMEM((every, width), BF16)] + [pltpu.VMEM((every, used), BF16)] * 3,
        cost_estimate=pl.CostEstimate(
            flops=2 * every * (width * 3 * used + 2 * heads * rows * used),
            bytes_accessed=every * width * 2 + 3 * used * width * 2 + every * used * 2,
            transcendentals=every * rows * heads,
        ),
    )


def add_mixed(places, keys, me_ref, w_hbm, resid_hbm, mixed_hbm, scratch):
    mixed_ref, w_ref, resid_ref, sems = scratch
    modules, share, _ = resid_ref.shape
    count = len(keys)
    copies = []
    for at, (place, key) in enumerate(zip(places, keys)):
        source = mixed_hbm[0].at[0] if place == 0 else mixed_hbm[place]
        pair = [
            pltpu.make_async_copy(source, mixed_ref.at[at], sems.at[2 * at]),
            pltpu.make_async_copy(
                w_hbm.at[holder(me_ref[0], key)], w_ref.at[at], sems.at[2 * at + 1]
            ),
        ]
        for copy in pair:
            copy.start()
        copies.append(pair)
    resid_copy = pltpu.make_async_copy(resid_hbm, resid_ref, sems.at[2 * count])
    resid_copy.start()
    total = None
    for at, pair in enumerate(copies):
        for copy in pair:
            copy.wait()
        term = dot_nn(mixed_ref[at], w_ref[at])
        total = term if total is None else total + term
    resid_copy.wait()
    return [resid_ref[m] + total[m * share : (m + 1) * share] for m in range(modules)]


def out_kernel(places, keys, me_ref, w_hbm, resid_hbm, *refs):
    mixed, (mid_ref, normed_ref), scratch = refs[:-6], refs[-6:-4], refs[-4:]
    modules = add_mixed(places, keys, me_ref, w_hbm, resid_hbm, mixed, scratch)
    for m, rows in enumerate(modules):
        mid_ref[m] = rows
        normed_ref[m] = rms_rows(rows).astype(BF16)


def add_split_kernel(keep_ref, got_ref, *out_refs):
    for at, out_ref in enumerate(out_refs):
        out_ref[...] = keep_ref[at] + got_ref[at]


def add_split(keep, got):
    count, *rest = keep.shape
    return launch(
        add_split_kernel,
        (keep, got),
        [WHOLE] * 2,
        out_shape=[shape_of(tuple(rest), F32)] * count,
        out_specs=[WHOLE] * count,
    )


def pool_kernel(resid_ref, *refs):
    modules = resid_ref.shape[0]
    total = functools.reduce(jnp.add, [resid_ref[m] for m in range(modules)])
    parts = functools.reduce(jnp.add, [ref[...] for ref in refs[:-1]])
    refs[-1][...] = rms_rows(total * (1.0 / modules) + parts).astype(BF16)


def pool(resid, parts):
    return launch(
        pool_kernel,
        (resid, *parts),
        [WHOLE] * (1 + len(parts)),
        out_shape=shape_of(parts[0].shape, BF16),
        out_specs=WHOLE,
    )


def out_call(kernel, me, keys, mixed, w_all, resid, out_shape, after=()):
    back = [(o, e) if e & 1 else (e, o) for e, o in keys]
    _, rows, inner = mixed[0].shape
    width = w_all.shape[-1]
    count = len(keys)
    return launch(
        functools.partial(kernel, [back.index(key) for key in keys], keys),
        (me, in_hbm(w_all), resid, *mixed),
        [SCALAR, ANYWHERE, ANYWHERE] + [ANYWHERE] * len(mixed),
        after,
        out_shape=out_shape,
        out_specs=[WHOLE] * len(out_shape),
        scratch_shapes=[
            pltpu.VMEM((count, rows, inner), BF16),
            pltpu.VMEM(w_all.shape, BF16),
            pltpu.VMEM(resid.shape, F32),
            pltpu.SemaphoreType.DMA((2 * count + 1,)),
        ],
        cost_estimate=pl.CostEstimate(
            flops=2 * rows * count * inner * width,
            bytes_accessed=count * inner * (width + rows) * 2 + rows * width * 10,
            transcendentals=0,
        ),
    )


def panel_table(w_disp_ref, hidden, with_log, slope_ref, norm):
    disp = dot_nt(w_disp_ref[...], hidden)
    slope_ref[...] = sigmoid(disp) * norm
    base = DISP_BASE + softplus(disp)
    parts = split3(base)
    if with_log:
        parts = [jnp.concatenate(pair, axis=1) for pair in zip(parts, split3(jnp.log(base)))]
    return jnp.concatenate([p.astype(F32) for p in parts], axis=0).astype(BF16)


def panel_pick(panel_ref, panel_count):
    genes = panel_ref.shape[0]
    over = lax.rem(lax.broadcasted_iota(jnp.int32, (genes, 3 * panel_count), 1), panel_count)
    return (panel_ref[...] == over).astype(F32).astype(BF16)


def place_cells(keys, me, blocks, hid_ref):
    share = blocks[0].shape[0]
    for key, block in zip(keys, blocks):
        hid_ref[pl.ds(holder(me, key) * share, share), :] = block


def rate_terms(logit, rate_scale, theta, seen, norm):
    small = jnp.exp(-jnp.abs(logit))
    soft = jnp.maximum(logit, 0.0) + jnp.log1p(small)
    rate = rate_scale * soft
    total = theta + rate
    above = theta * (rate - seen) * jnp.where(logit >= 0.0, norm, norm * small)
    d_logit = above / (soft * total * (1.0 + small))
    return rate, total, d_logit


def decode_kernel(
    keys, norm, me_ref, counts_ref, col_ref, row_ref, scale_ref, wm_ref, wd_ref, *refs
):
    hids = refs[: len(keys)]
    high_ref, low_ref, sum_ref, hid_ref, slope_ref, table_ref = refs[len(keys) :]
    cells = hid_ref.shape[0]
    panel_count = wd_ref.shape[0]

    @pl.when(pl.program_id(0) == 0)
    def _():
        place_cells(keys, me_ref[0], [block[...] for block in hids], hid_ref)
        table_ref[...] = panel_table(wd_ref, hid_ref[...], True, slope_ref, norm)
        sum_ref[...] = jnp.zeros_like(sum_ref)

    both = dot_nn(panel_pick(col_ref, panel_count), table_ref[...])
    theta, log_theta = both[:, :cells], both[:, cells:]
    seen = counts_ref[...].astype(F32)
    rate, total, d_logit = rate_terms(
        dot_nt(wm_ref[...], hid_ref[...]), scale_ref[...], theta, seen, norm
    )
    high_ref[...], low_ref[...] = split2(d_logit)
    log_total = jnp.log(total)
    product = jnp.ones_like(theta)
    slope = jnp.zeros_like(theta)
    for k in range(COUNT_MOST):
        inverse = 1.0 / (k + 1.0)
        factor = theta * inverse + k * inverse
        here = seen > k
        slope = jnp.where(here, slope * factor + product * inverse, slope)
        product = jnp.where(here, product * factor, product)
    nll = -(
        jnp.log(product)
        + theta * (log_theta - log_total)
        + seen * (jnp.log(rate) - log_total)
    )
    d_theta = -(slope / product + log_theta + 1.0 - log_total - (theta + seen) / total)
    down = lax.broadcasted_iota(jnp.int32, (panel_count, theta.shape[0]), 0)
    pick = (down == row_ref[0]).astype(F32).astype(BF16)
    high, middle, low = split3(d_theta)
    sum_ref[:panel_count, :] += dot_nn(pick, high) + dot_nn(pick, middle) + dot_nn(pick, low)
    sum_ref[panel_count : panel_count + 1, :] += jnp.sum(nll, axis=0, keepdims=True)


def decode(me, keys, counts_t, panel_col, panel_row, rate_scale, w_mean_t, w_disp_t, hids, norm):
    genes, cells = counts_t.shape
    width = w_mean_t.shape[1]
    panel_count = w_disp_t.shape[0]
    steps, _, tile = panel_row.shape
    wide = -(-(panel_count + 1) // 8) * 8
    by_gene = lambda columns: pl.BlockSpec((tile, columns), lambda i: (i, 0))
    return launch(
        functools.partial(decode_kernel, keys, norm),
        (
            me,
            counts_t,
            panel_col,
            panel_row,
            rate_scale,
            in_hbm(w_mean_t),
            w_disp_t,
            *hids,
        ),
        [
            SCALAR,
            by_gene(cells),
            by_gene(1),
            pl.BlockSpec((1, 1, tile), lambda i: (i, 0, 0)),
            fixed(1, cells),
            by_gene(width),
            fixed(panel_count, width),
        ]
        + [fixed(*hids[0].shape)] * len(hids),
        grid=(steps,),
        out_shape=(
            shape_of((genes, cells), BF16),
            shape_of((genes, cells), BF16),
            shape_of((wide, cells), F32),
            shape_of((cells, width), BF16),
            shape_of((panel_count, cells), F32),
        ),
        out_specs=[
            by_gene(cells),
            by_gene(cells),
            fixed(wide, cells),
            fixed(cells, width),
            fixed(panel_count, cells),
        ],
        scratch_shapes=[pltpu.VMEM((3 * panel_count, 2 * cells), BF16)],
        cost_estimate=pl.CostEstimate(
            flops=2 * genes * cells * width + 150 * genes * cells,
            bytes_accessed=genes * (width * 2 + cells * 8),
            transcendentals=8 * genes * cells,
        ),
    )


def far_kernel(keys, norm, genes_all, place_ref, seen_ref, lib_ref, col_ref, wm_ref, wd_ref, *refs):
    hids = refs[:2]
    high_ref, low_ref, hid_ref, slope_ref, table_ref = refs[2:]
    seen = seen_ref[0].astype(F32)
    lib = lib_ref[0].astype(F32)
    panel_count = wd_ref.shape[0]

    @pl.when(pl.program_id(0) == 0)
    def _():
        blocks = [half[at, 0] for half in hids for at in range(half.shape[0])]
        place_cells(keys, place_ref[0], blocks, hid_ref)
        table_ref[...] = panel_table(wd_ref, hid_ref[...], False, slope_ref, norm)

    library = jnp.sum(lib, axis=0, keepdims=True)
    _, _, d_logit = rate_terms(
        dot_nt(wm_ref[...], hid_ref[...]),
        library / genes_all,
        dot_nn(panel_pick(col_ref, panel_count), table_ref[...]),
        seen,
        norm,
    )
    high_ref[...], low_ref[...] = split2(d_logit)


def far_call(place, keys, other, seen, panel_col, w_mean_t, w_disp_t, hids, norm, genes_all):
    genes, width = w_mean_t.shape
    cells = seen.shape[2]
    panel_count = w_disp_t.shape[0]
    near, _, share, _ = hids[0].shape
    tile = tile_of(genes, 16, 256)
    by_gene = lambda columns: pl.BlockSpec((tile, columns), lambda i, at: (i, 0))
    last = genes // EXTRA
    return pl.pallas_call(
        functools.partial(far_kernel, keys, norm, genes_all),
        grid_spec=pltpu.PrefetchScalarGridSpec(
            num_scalar_prefetch=1,
            grid=(genes // tile,),
            in_specs=[
                pl.BlockSpec((1, tile, cells), lambda i, at: (at[1] ^ other, i, 0)),
                pl.BlockSpec((1, EXTRA, cells), lambda i, at: (at[1] ^ other, last, 0)),
                by_gene(1),
                by_gene(width),
                pl.BlockSpec((panel_count, width), lambda i, at: (0, 0)),
            ]
            + [pl.BlockSpec((near, 1, share, width), lambda i, at: (0, other - 1, 0, 0))]
            * len(hids),
            out_specs=[
                by_gene(cells),
                by_gene(cells),
                pl.BlockSpec((cells, width), lambda i, at: (0, 0)),
                pl.BlockSpec((panel_count, cells), lambda i, at: (0, 0)),
            ],
            scratch_shapes=[pltpu.VMEM((3 * panel_count, cells), BF16)],
        ),
        out_shape=(
            shape_of((genes, cells), BF16),
            shape_of((genes, cells), BF16),
            shape_of((cells, width), BF16),
            shape_of((panel_count, cells), F32),
        ),
        compiler_params=PARAMS,
        cost_estimate=pl.CostEstimate(
            flops=2 * genes * cells * width + 60 * genes * cells,
            bytes_accessed=genes * (width * 2 + cells * 6),
            transcendentals=4 * genes * cells,
        ),
    )(place, seen, seen, panel_col, in_hbm(w_mean_t), w_disp_t, *hids)


def grad_kernel(place_ref, *refs):
    out_ref = refs[-1]
    mine, width = out_ref.shape[0], refs[0].shape[1]
    down = lax.broadcasted_iota(jnp.int32, (mine, width), 0) + place_ref[1] * mine
    over = lax.broadcasted_iota(jnp.int32, (mine, width), 1)
    pick = (down == over).astype(F32).astype(BF16)
    total = None
    for at in range(0, len(refs) - 1, 3):
        hidden = dot_nt(pick, refs[at][...]).astype(BF16)
        term = dot_nt(hidden, refs[at + 1][...]) + dot_nt(hidden, refs[at + 2][...])
        total = term if total is None else total + term
    out_ref[...] = total


def grad_mean_call(place, groups):
    cells, width = groups[0][0].shape
    genes = groups[0][1].shape[0]
    mine = width // len(groups)
    return launch(
        grad_kernel,
        (place, *[array for group in groups for array in group]),
        [SCALAR] + [WHOLE] * 3 * len(groups),
        params=LARGE,
        out_shape=shape_of((mine, genes), F32),
        out_specs=WHOLE,
        cost_estimate=pl.CostEstimate(
            flops=2 * len(groups) * cells * mine * (width + 2 * genes),
            bytes_accessed=len(groups) * cells * (width + 2 * genes) * 2 + mine * genes * 4,
            transcendentals=0,
        ),
    )


def disp_kernel(genes_all, place_ref, *refs):
    count = (len(refs) - 3) // 3
    sums, hids, slopes = refs[:count], refs[count : 2 * count], refs[2 * count : 3 * count]
    grad_ref, loss_ref, term_ref = refs[3 * count :]
    panel_count = grad_ref.shape[0]
    for other in range(count):
        hidden = hids[other][...]
        d_disp = sums[other][:panel_count] * slopes[other][...]
        parts = jnp.concatenate([part.astype(F32) for part in split3(d_disp)], axis=0)
        three = dot_nn(parts.astype(BF16), hidden)
        term_ref[place_ref[1] ^ other] = (
            three[:panel_count]
            + three[panel_count : 2 * panel_count]
            + three[2 * panel_count :]
        )
    total = term_ref[0]
    for block in range(1, count):
        total = total + term_ref[block]
    grad_ref[...] = total
    loss_ref[...] = sums[0][panel_count : panel_count + 1] * (1.0 / genes_all)


def disp_call(place, sums, hids, slopes, genes_all, after):
    panel_count, cells = slopes[0].shape
    width = hids[0].shape[1]
    return launch(
        functools.partial(disp_kernel, genes_all),
        (place, *sums, *hids, *slopes),
        [SCALAR] + [WHOLE] * 3 * len(sums),
        after,
        out_shape=(shape_of((panel_count, width), F32), shape_of((1, cells), F32)),
        out_specs=[WHOLE] * 2,
        scratch_shapes=[pltpu.VMEM((len(sums), panel_count, width), F32)],
    )


def pack_kernel(counts_ref, library_ref, out_ref):
    genes, cells = counts_ref.shape
    out_ref[:genes, :] = counts_ref[...].astype(F32).astype(BF16)
    parts = [part.astype(F32) for part in split3(library_ref[...])]
    parts.append(jnp.zeros((EXTRA - len(parts), cells), F32))
    out_ref[genes:, :] = jnp.concatenate(parts, axis=0).astype(BF16)


def pack(counts_t, library, after):
    genes, cells = counts_t.shape
    return launch(
        pack_kernel,
        (counts_t, library),
        [WHOLE] * 2,
        after,
        out_shape=shape_of((genes + EXTRA, cells), BF16),
        out_specs=WHOLE,
    )


def add_kernel(left_ref, right_ref, out_ref):
    out_ref[...] = left_ref[...] + right_ref[...]


def add(left, right, after):
    return launch(
        add_kernel,
        (left, right),
        [WHOLE] * 2,
        after,
        out_shape=shape_of(left.shape, left.dtype),
        out_specs=WHOLE,
    )


def stack_kernel(*refs):
    for at, ref in enumerate(refs[:-1]):
        refs[-1][at] = ref[...]


def stack(parts, after):
    return launch(
        stack_kernel,
        parts,
        [WHOLE] * len(parts),
        after,
        out_shape=shape_of((len(parts),) + parts[0].shape, parts[0].dtype),
        out_specs=WHOLE,
    )


def flat_qkv(weights):
    return weights.transpose(2, 1, 0).reshape(-1, weights.shape[0])


def flat_out(weights):
    return weights.transpose(1, 0, 2).reshape(-1, weights.shape[2])


def shards(
    counts,
    panels,
    membership,
    w_proj,
    w_qkv_within,
    w_out_within,
    w_qkv_cross,
    w_out_cross,
    w_mean,
    w_disp,
):
    cells, genes_here = counts.shape
    width, heads, triple = w_qkv_within.shape
    head_width = triple // 3
    modules = w_proj.shape[1] // width
    gene_count = lax.axis_size("gene")
    grp_count = lax.axis_size("grp")
    genes_all = genes_here * gene_count
    share = cells // gene_count
    panel_count = w_disp.shape[1]
    norm = float(cells * grp_count) ** (-0.5)
    gene_me = lax.axis_index("gene").astype(jnp.int32)
    grp_me = lax.axis_index("grp").astype(jnp.int32)
    me = gene_me.reshape(1)
    place = jnp.stack([gene_me, grp_me])
    keys = spread_keys(gene_count)
    far = far_keys(gene_count)

    counts_t = counts.T
    w_mean_t = w_mean.T
    w_disp_t = w_disp.T

    library = jnp.sum(counts_t.astype(F32), axis=0, keepdims=True)
    for bit in range(gene_count.bit_length() - 1):
        library = library + hop(library, "gene", straight(1 << bit))
    library = 1.0 + library
    flat_within = flat_qkv(w_qkv_within)
    flat_cross = flat_qkv(w_qkv_cross)
    out_within = in_hbm(lax.all_gather(flat_out(w_out_within), "gene"))
    out_cross = flat_out(w_out_cross)
    cell_ids = jnp.tile(jnp.arange(share, dtype=jnp.int32), modules)
    odd = (gene_me & 1) == 1
    owners = gene_me ^ jnp.where(odd, jnp.array([o for _, o in keys]), jnp.array([e for e, _ in keys]))
    group_ids = jnp.take(membership.reshape(gene_count, share), owners, axis=0).reshape(-1)
    cell_ids = (cell_ids.reshape(-1, 1), cell_ids.reshape(1, -1))
    group_ids = (group_ids.reshape(-1, 1), group_ids.reshape(1, -1))
    tile = tile_of(genes_here, 16, 256)
    panel_col = panels.reshape(genes_here, 1)
    panel_row = panels.reshape(genes_here // tile, 1, tile)

    halves = []
    early = [*cell_ids, *group_ids, panel_col, panel_row]
    for chunk in range(2):
        keep, send = project(me, counts_t, TARGET / library, w_proj, keys, chunk, 2, early)
        early = []
        halves.append((keep, hop(send, "gene", straight(1))))
    laid = [[flat_within], [flat_cross, out_cross]]
    for at, key in enumerate(far[::-1]):
        nexts = []
        for chunk, (keep, got) in enumerate(halves):
            keep, send = halve(keep, got, laid[chunk] if at == 1 else ())
            nexts.append((keep, hop(send, "gene", key)))
        halves = nexts
    resid, normed = to_rows(halves, width)

    packed = pack(counts_t, library, [resid])
    seen = in_hbm(lax.all_gather(packed, "grp"))
    normed = stack([normed], [out_within, packed])[0]

    in_cell = [[(block, m) for m in range(modules)] for block in range(gene_count)]
    across = [[(block, m) for block in range(gene_count)] for m in range(modules)]

    def send_mixed(mixed):
        return [mixed] + [hop(mixed[at], "gene", keys[at]) for at in range(1, gene_count)]

    blocks = spread(normed, "gene")
    (mixed,) = attend(blocks, flat_within, cell_ids, in_cell, heads, head_width)
    rows = (modules, share, width)
    mid, normed = out_call(
        out_kernel,
        me,
        keys,
        send_mixed(mixed),
        out_within,
        resid,
        [shape_of(rows, F32), shape_of(rows, BF16)],
    )

    normed = stack([normed], [seen])[0]

    keep, send = attend(
        spread(normed, "gene"), flat_cross, group_ids, across, heads, head_width, out_cross
    )
    got = hop(send, "gene", straight(1))
    parts = list(add_split(keep, got))
    parts = parts[:1] + [hop(part, "gene", key) for part, key in zip(parts[1:], keys[1:])]
    hidden = pool(mid, parts)

    away = [hop(hidden, "grp", straight(rel)) for rel in range(1, grp_count)]
    own = stack([hidden], away[:2])[0]
    hids = [own] + [hop(own, "gene", key) for key in keys[1 : gene_count // 2]]
    hids += [hop(block, "gene", straight(1)) for block in hids]
    far_hids = [stack(away, [])]
    far_hids += [hop(far_hids[0], "gene", key) for key in keys[1 : gene_count // 2]]
    high, low, sums, own_hid, slope = decode(
        me, keys, counts_t, panel_col, panel_row, library / genes_all, w_mean_t, w_disp_t, hids, norm
    )
    groups = [(own_hid, high, low)]
    slopes = [slope]
    far_hids = [stack(far_hids, [high])]
    far_hids.append(hop(far_hids[0], "gene", straight(1)))
    for other in range(1, grp_count):
        high, low, hid, slope = far_call(
            place, keys, other, seen, panel_col, w_mean_t, w_disp_t, far_hids, norm, genes_all
        )
        groups.append((hid, high, low))
        slopes.append(slope)
    bits = gene_count.bit_length() - 1
    for bit in range(bits):
        after = [groups[min(bit, grp_count - 1)][1]]
        sums = add(sums, hop(sums, "gene", straight(1 << bit)), after)
    sums = [sums] + [hop(sums, "grp", straight(rel)) for rel in range(1, grp_count)]
    grad_mean = in_hbm(grad_mean_call(place, groups))
    grad_disp, loss = disp_call(
        place, sums, [group[0] for group in groups], slopes, genes_all, [grad_mean]
    )
    return (loss.reshape(cells), grad_mean, grad_disp.T)


def solution(mesh):
    return jax.shard_map(
        shards,
        mesh=mesh,
        in_specs=(
            P("grp", "gene"),
            P("gene"),
            P("grp", None),
            P("gene", None),
            P(None, "gene", None),
            P("gene", None, None),
            P(None, "gene", None),
            P("gene", None, None),
            P(None, "gene"),
            P(),
        ),
        out_specs=(P("grp"), P("grp", "gene"), P()),
        check_vma=False,
    )
```
